32 devices in a mesh: inp: 8 (over z, y), vis: 4 (over x, core).
Axes of the slice: x: 2, y: 2, z: 4, core: 2. Of those that a mesh axis runs over, the one named last changes fastest.
Arguments:
- samples: bfloat16 [128, 2048, 2048], P('vis', 'inp'), may hold values from -6 to 6
- history: bfloat16 [3, 2048, 2048], P(None, 'inp'), may hold values from -6 to 6
- fir_taps: float32 [4, 2048], replicated, may hold values from -3 to 3
- kept_channels: int32 [8], replicated, may hold values from 0 to 1023, as said below
Outputs:
- visibility: bfloat16 [8, 2048, 2048], P('inp', 'vis')
The draws below stay inside these ranges and needn't reach their ends.
Inputs may be any that keep to these rules, and one draw needn't show every extreme that they name: `kept_channels`: 8 distinct channel numbers in no particular order; channels 0 and 1023 are always among them.
All inputs are finite; a program needn't handle non-finite values.
Results may differ from the reference program's by a relative error of at most 0.0078.
Values may be sent and summed in bfloat16 or wider, within the bound.
No kernel may reach another device: no remote copies, remote signals or barrier semaphores. Data moves between devices by JAX's collectives and lax.ppermute only.
A program may use at most 128 MiB of HBM per device.

```python
import math
import jax
import jax.numpy as jnp
from jax import lax

INPUTS = 2048
CHANNELS = 1024
TAPS = 4
SAMPLES = 2048
KEEP = 8
FRAMES = 128


def draw_kept_channels(key, part):
    inner = jax.random.permutation(key, CHANNELS - 2)[:KEEP - 2].astype(jnp.int32) + 1
    chosen = jnp.concatenate([jnp.array([0, CHANNELS - 1], jnp.int32), inner])
    return jax.random.permutation(jax.random.fold_in(key, 7), chosen).astype(jnp.int32)


def block_scale(own_key, extent, pieces, least, high):
    def one(axis_at, blocks):
        heights = jax.random.uniform(jax.random.fold_in(jax.random.fold_in(own_key, 6), axis_at), (blocks,), jnp.float32, least / len(pieces), high / len(pieces))
        return jnp.repeat(jnp.exp(heights), extent[axis_at] // blocks).reshape((-1,) + (1,) * (len(extent) - axis_at - 1))

    gain = one(*pieces[0])
    for cut in pieces[1:]:
        gain = gain * one(*cut)
    return gain


def centred(key, shape, spread, most, cuts=(), held_as=jnp.bfloat16):
    drawn = spread * jax.random.normal(key, shape, jnp.float32)
    if cuts:
        drawn = drawn * block_scale(key, shape, cuts, -0.22, 0.18)
    return jnp.clip(drawn, -most, most).astype(held_as)


def setup_inputs(seed: int = 0) -> dict:
    splits = jax.random.split(jax.random.key(seed), 5)
    samples = centred(splits[0], (FRAMES, INPUTS, SAMPLES), 1.0, 6.0, ((0, 4), (1, 8)))
    history = centred(splits[1], (TAPS - 1, INPUTS, SAMPLES), 1.0, 6.0, ((1, 8),))
    fir_taps = centred(splits[2], (TAPS, SAMPLES), 0.5, 3.0, (), jnp.float32)
    kept_channels = draw_kept_channels(jax.random.fold_in(splits[4], 71), 0)
    return dict(samples=samples, history=history, fir_taps=fir_taps, kept_channels=kept_channels)


def make_table(kept_channels, sample_count):
    positions = jnp.arange(sample_count, dtype=jnp.int32)
    products = kept_channels.astype(jnp.int32)[:, None] * positions[None, :] % sample_count
    angles = products.astype(jnp.float32) * (2.0 * math.pi / sample_count)
    norm_scale = 1.0 / math.sqrt(sample_count)
    table = jnp.concatenate([jnp.cos(angles) * norm_scale, -jnp.sin(angles) * norm_scale], axis=0)
    return table.astype(jnp.bfloat16)

def reference(samples, history, fir_taps, kept_channels):
    dft_table = make_table(kept_channels, SAMPLES)

    def one_frame(frame):
        weighted = jnp.zeros((INPUTS, SAMPLES), jnp.float32)
        for tap_index in range(TAPS):
            source = frame - (TAPS - 1) + tap_index
            from_window = lax.dynamic_index_in_dim(samples, jnp.maximum(source, 0).astype(jnp.int32), 0, keepdims=False)
            from_history = lax.dynamic_index_in_dim(history, jnp.clip(source + TAPS - 1, 0, TAPS - 2).astype(jnp.int32), 0, keepdims=False)
            chosen = jnp.where(source >= 0, from_window, from_history)
            weighted = weighted + fir_taps[tap_index][None, :] * chosen.astype(jnp.float32)
        weighted = weighted.astype(jnp.bfloat16)
        return jnp.dot(dft_table, weighted.T, preferred_element_type=jnp.float32).astype(jnp.bfloat16)
    spectra = lax.map(one_frame, jnp.arange(FRAMES, dtype=jnp.int32))

    def one_channel(channel):
        real_part = lax.dynamic_index_in_dim(spectra, channel, 1, keepdims=False)
        imag_part = lax.dynamic_index_in_dim(spectra, channel + KEEP, 1, keepdims=False)
        re_sum = jnp.dot(real_part.T, real_part, preferred_element_type=jnp.float32) + jnp.dot(imag_part.T, imag_part, preferred_element_type=jnp.float32)
        im_sum = jnp.dot(imag_part.T, real_part, preferred_element_type=jnp.float32) - jnp.dot(real_part.T, imag_part, preferred_element_type=jnp.float32)
        row_ids = jnp.arange(INPUTS, dtype=jnp.int32)
        upper = row_ids[None, :] >= row_ids[:, None]
        return (jnp.where(upper, re_sum, im_sum) / float(FRAMES)).astype(jnp.bfloat16)
    return lax.map(one_channel, jnp.arange(KEEP, dtype=jnp.int32))
```

```python
import math

import jax
import jax.numpy as jnp
from jax import lax
from jax.experimental import pallas as pl
from jax.experimental.pallas import tpu as pltpu
from jax.sharding import PartitionSpec as P

TAPS = 4
CHUNK = 2
ROW_TILE = 128
COL_TILE = 256
LANES = 128
MIB = 1024 * 1024


def build_table(kept_ref, taps_ref, dft, wide):
    kept_total = kept_ref.shape[0]
    sample_count = taps_ref.shape[1]
    positions = lax.broadcasted_iota(jnp.int32, (1, sample_count), 1)
    norm_scale = 1.0 / math.sqrt(sample_count)
    step = 2.0 * math.pi / sample_count
    products = jnp.concatenate([lax.rem(kept_ref[c] * positions, sample_count) for c in range(kept_total)], axis=0)
    angles = products.astype(jnp.float32) * step
    dft[0:kept_total] = jnp.cos(angles) * norm_scale
    dft[kept_total:] = -jnp.sin(angles) * norm_scale
    rounded = dft[...].astype(jnp.bfloat16).astype(jnp.float32)
    high_parts, low_parts = [], []
    for tap in reversed(range(TAPS)):
        scaled = rounded * taps_ref[tap : tap + 1, :]
        high = scaled.astype(jnp.bfloat16).astype(jnp.float32)
        high_parts.append(high)
        low_parts.append(scaled - high)
    columns = jnp.concatenate(high_parts + low_parts, axis=0)
    wide[...] = columns.T.astype(jnp.bfloat16)


def spectra_kernel(kept_ref, taps_ref, samples_ref, history_ref, out_ref, held, past, dft, wide, sums, sems, past_sem):
    frame_count, input_count, sample_count = samples_ref.shape
    kept_total = kept_ref.shape[0]
    rows = 2 * kept_total
    lead = TAPS - 1
    chunk_total = frame_count // CHUNK
    first_block = lax.axis_index("vis") == 0

    def chunk_copy(index):
        part = pl.ds(index * CHUNK, CHUNK)
        return pltpu.make_async_copy(samples_ref.at[part], held.at[part], sems.at[index])

    past_copy = pltpu.make_async_copy(history_ref, past, past_sem)

    @pl.when(first_block)
    def _():
        past_copy.start()

    for index in range(chunk_total):
        chunk_copy(index).start()

    build_table(kept_ref, taps_ref, dft, wide)
    sums[...] = jnp.zeros_like(sums)

    def add_frame(block, slot):
        turned = block.T
        both = turned[: TAPS * rows] + turned[TAPS * rows :]
        place = pl.ds(pl.multiple_of(slot * rows, 8), TAPS * rows)
        for h in range(input_count // LANES):
            sums[h, place, :] = sums[h, place, :] + both[:, h * LANES : (h + 1) * LANES]

    @pl.when(first_block)
    def _():
        past_copy.wait()
        for k in range(lead):
            add_frame(jnp.dot(past[k], wide[...], preferred_element_type=jnp.float32), k)

    @pl.loop(0, chunk_total)
    def _(index):
        chunk_copy(index).wait()
        block = held[pl.ds(index * CHUNK, CHUNK)].reshape(CHUNK * input_count, sample_count)
        products = jnp.dot(block, wide[...], preferred_element_type=jnp.float32)
        for k in range(CHUNK):
            add_frame(products[k * input_count : (k + 1) * input_count], index * CHUNK + k + lead)

    halo_rows = lax.broadcasted_iota(jnp.int32, (8, LANES), 0)
    end = lead + frame_count
    for c in range(kept_total):
        for h in range(input_count // LANES):
            cols = slice(h * LANES, (h + 1) * LANES)
            for part in range(2):
                first = lead * rows + part * kept_total + c
                column = sums[h, pl.ds(first, frame_count, stride=rows), :]
                out_ref[c, part * frame_count : (part + 1) * frame_count, cols] = column.astype(jnp.bfloat16)
            real_tail = sums[h, pl.ds(end * rows + c, 8, stride=rows), :]
            imag_tail = sums[h, pl.ds((end - lead) * rows + kept_total + c, 8, stride=rows), :]
            tail = jnp.where(halo_rows < lead, real_tail, jnp.where(halo_rows < 2 * lead, imag_tail, 0.0))
            out_ref[c, 2 * frame_count :, cols] = tail.astype(jnp.bfloat16)


def spectra_part(samples, history, fir_taps, kept_channels):
    frame_count, input_count, sample_count = samples.shape
    kept_total = kept_channels.shape[0]
    rows = 2 * kept_total
    lead = TAPS - 1
    any_space = pl.BlockSpec(memory_space=pl.ANY)
    return pl.pallas_call(
        spectra_kernel,
        out_shape=jax.ShapeDtypeStruct((kept_total, 2 * frame_count + 8, input_count), jnp.bfloat16),
        in_specs=[
            pl.BlockSpec(memory_space=pltpu.SMEM),
            pl.BlockSpec(memory_space=pltpu.VMEM),
            any_space,
            any_space,
        ],
        out_specs=pl.BlockSpec(memory_space=pltpu.VMEM),
        scratch_shapes=[
            pltpu.VMEM((frame_count, input_count, sample_count), jnp.bfloat16),
            pltpu.VMEM((lead, input_count, sample_count), jnp.bfloat16),
            pltpu.VMEM((rows, sample_count), jnp.float32),
            pltpu.VMEM((sample_count, 2 * TAPS * rows), jnp.bfloat16),
            pltpu.VMEM((input_count // LANES, (frame_count + lead + 8) * rows, LANES), jnp.float32),
            pltpu.SemaphoreType.DMA((frame_count // CHUNK,)),
            pltpu.SemaphoreType.DMA,
        ],
        compiler_params=pltpu.CompilerParams(vmem_limit_bytes=52 * MIB),
    )(kept_channels, fir_taps, samples, history)


def correlate_kernel(own_ref, core_ref, chip_ref, far_ref, out_ref, pair, halos, *, frame_count, scale):
    step = pl.program_id(0)
    me = lax.axis_index("vis")
    sources, _, input_count = own_ref.shape
    input_total = sources * input_count
    lead = TAPS - 1
    row_count = out_ref.shape[1] * pl.num_programs(0)
    parts = (own_ref, core_ref, chip_ref, far_ref)

    @pl.when(step == 0)
    def _():
        for k, part in enumerate(parts):
            for s in range(sources):
                halos[me ^ k, :, s * input_count : (s + 1) * input_count] = part[s, 2 * frame_count :, :]
        halo_rows = lax.broadcasted_iota(jnp.int32, (8, input_total), 0)
        for k, part in enumerate(parts):
            block = me ^ k
            before = jnp.maximum(block - 1, 0)
            halo = halos[before].astype(jnp.float32)
            halo = jnp.where(block > 0, halo, 0.0)
            real_halo = jnp.where(halo_rows < lead, halo, 0.0)
            imag_halo = jnp.where(halo_rows < lead, pltpu.roll(halo, 8 - lead, 0), 0.0)
            for s in range(sources):
                cols = slice(s * input_count, (s + 1) * input_count)
                real = part[s, :frame_count, :].astype(jnp.float32)
                imag = part[s, frame_count : 2 * frame_count, :].astype(jnp.float32)
                real = jnp.concatenate([real[:8] + real_halo[:, cols], real[8:]], axis=0)
                imag = jnp.concatenate([imag[:8] + imag_halo[:, cols], imag[8:]], axis=0)
                base = k * 2 * frame_count
                pair[0, base : base + frame_count, cols] = real.astype(jnp.bfloat16)
                pair[0, base + frame_count : base + 2 * frame_count, cols] = imag.astype(jnp.bfloat16)
                pair[1, base : base + frame_count, cols] = (-imag).astype(jnp.bfloat16)
                pair[1, base + frame_count : base + 2 * frame_count, cols] = real.astype(jnp.bfloat16)

    first_row = pl.multiple_of(me * row_count + step * ROW_TILE, ROW_TILE)
    left = pair[0, :, pl.ds(first_row, ROW_TILE)].T

    def product(which, cols):
        return jnp.dot(left, pair[which, :, cols], preferred_element_type=jnp.float32) * scale

    for j in range(input_total // COL_TILE):
        cols = slice(j * COL_TILE, (j + 1) * COL_TILE)
        below = (j * COL_TILE < first_row).astype(jnp.int32)
        out_ref[0, :, cols] = product(below, cols).astype(jnp.bfloat16)

    corner = pl.multiple_of(first_row // COL_TILE * COL_TILE, COL_TILE)
    cols = pl.ds(corner, COL_TILE)
    row_ids = first_row + lax.broadcasted_iota(jnp.int32, (ROW_TILE, COL_TILE), 0)
    col_ids = corner + lax.broadcasted_iota(jnp.int32, (ROW_TILE, COL_TILE), 1)
    mixed = jnp.where(col_ids >= row_ids, product(0, cols), product(1, cols))
    out_ref[0, :, cols] = mixed.astype(jnp.bfloat16)


def correlate_part(parts, frame_count, row_count):
    sources, _, input_count = parts[0].shape
    input_total = sources * input_count
    block_total = len(parts)
    depth = 2 * frame_count * block_total
    return pl.pallas_call(
        lambda *refs: correlate_kernel(*refs, frame_count=frame_count, scale=1.0 / (frame_count * block_total)),
        grid=(row_count // ROW_TILE,),
        out_shape=jax.ShapeDtypeStruct((1, row_count, input_total), jnp.bfloat16),
        in_specs=[pl.BlockSpec(memory_space=pltpu.VMEM)] * block_total,
        out_specs=pl.BlockSpec((1, ROW_TILE, input_total), lambda g: (0, g, 0)),
        scratch_shapes=[
            pltpu.VMEM((2, depth, input_total), jnp.bfloat16),
            pltpu.VMEM((block_total, 8, input_total), jnp.bfloat16),
        ],
        compiler_params=pltpu.CompilerParams(vmem_limit_bytes=32 * MIB),
    )(*parts)


def exchanged(value, distance):
    count = lax.axis_size("vis")
    return lax.ppermute(value, "vis", [(source, source ^ distance) for source in range(count)])


def per_device(samples, history, fir_taps, kept_channels):
    vis_count = lax.axis_size("vis")
    inp_count = lax.axis_size("inp")
    frame_count, input_count, _ = samples.shape
    spectra = spectra_part(samples, history, fir_taps, kept_channels)
    own = lax.all_to_all(spectra, "inp", split_axis=0, concat_axis=0, tiled=True)
    chip = exchanged(own, 2)
    core = exchanged(own, 1)
    far = exchanged(chip, 1)
    return correlate_part((own, core, chip, far), frame_count, input_count * inp_count // vis_count)


def shifted(value, axis, steps):
    count = lax.axis_size(axis)
    initial, last = (max(0, -steps), min(count, count - steps))
    return lax.ppermute(value, axis, [(source, source + steps) for source in range(initial, last)])


def make_table(kept_channels, sample_count):
    positions = jnp.arange(sample_count, dtype=jnp.int32)
    products = kept_channels[:, None] * positions[None, :] % sample_count
    angles = products.astype(jnp.float32) * (2.0 * math.pi / sample_count)
    norm_scale = 1.0 / math.sqrt(sample_count)
    table = jnp.concatenate([jnp.cos(angles) * norm_scale, -jnp.sin(angles) * norm_scale], axis=0)
    return table.astype(jnp.bfloat16)


def per_device_plain(samples, history, fir_taps, kept_channels):
    vis_count = lax.axis_size("vis")
    vis_index = lax.axis_index("vis")
    inp_count = lax.axis_size("inp")
    frame_count, input_count, sample_count = samples.shape
    kept_total = kept_channels.shape[0]
    previous = shifted(samples[frame_count - TAPS + 1 :], "vis", 1)
    previous = jnp.where(vis_index == 0, history, previous)
    extended = jnp.concatenate([previous, samples], axis=0).astype(jnp.float32)
    weighted = fir_taps[0] * extended[0:frame_count]
    for tap in range(1, TAPS):
        weighted = weighted + fir_taps[tap] * extended[tap : tap + frame_count]
    spectra = jnp.einsum(
        "kn,fin->kfi",
        make_table(kept_channels, sample_count),
        weighted.astype(jnp.bfloat16),
        preferred_element_type=jnp.float32,
    ).astype(jnp.bfloat16)
    spectra = spectra.reshape(2, kept_total, frame_count, input_count)
    mine = lax.all_to_all(spectra, "inp", split_axis=1, concat_axis=3, tiled=True)
    mine = lax.all_gather(mine, "vis", axis=2, tiled=True)
    real, imag = mine[0], mine[1]
    stacked = jnp.concatenate([real, imag], axis=1)
    rotated = jnp.concatenate([-imag, real], axis=1)
    input_total = input_count * inp_count
    row_count = input_total // vis_count
    left = lax.dynamic_slice_in_dim(stacked, vis_index * row_count, row_count, 2)
    re_block = jnp.einsum("cfa,cfb->cab", left, stacked, preferred_element_type=jnp.float32)
    im_block = jnp.einsum("cfa,cfb->cab", left, rotated, preferred_element_type=jnp.float32)
    row_ids = vis_index * row_count + jnp.arange(row_count, dtype=jnp.int32)
    col_ids = jnp.arange(input_total, dtype=jnp.int32)
    packed = jnp.where(col_ids[None, None, :] >= row_ids[None, :, None], re_block, im_block)
    return (packed / float(frame_count * vis_count)).astype(jnp.bfloat16)


def solution(mesh):
    def run(samples, history, fir_taps, kept_channels):
        input_count = samples.shape[1] // mesh.shape["inp"]
        row_count = samples.shape[1] // mesh.shape["vis"]
        one_channel = kept_channels.shape[0] == mesh.shape["inp"]
        tiled = input_count % 128 == 0 and row_count % ROW_TILE == 0 and mesh.shape["vis"] == 4 and one_channel
        return jax.shard_map(
            per_device if tiled else per_device_plain,
            mesh=mesh,
            in_specs=(P("vis", "inp", None), P(None, "inp", None), P(), P()),
            out_specs=P("inp", "vis", None),
            check_vma=False,
        )(samples, history, fir_taps, kept_channels)

    return run
```

```python
import math

import jax
import jax.numpy as jnp
from jax import lax
from jax.experimental import pallas as pl
from jax.experimental.pallas import tpu as pltpu
from jax.sharding import PartitionSpec as P

TAPS = 4
CHUNK = 4
WINDOW = 3
ROW_TILE = 128
COL_TILE = 256
LANES = 128
MIB = 1024 * 1024


def build_table(kept_ref, taps_ref, columns, wide):
    kept_total = kept_ref.shape[0]
    rows = 2 * kept_total
    count = taps_ref.shape[1]
    quarter = count // 4
    row_ids = lax.broadcasted_iota(jnp.int32, (kept_total, count), 0)
    positions = lax.broadcasted_iota(jnp.int32, (kept_total, count), 1)
    channels = jnp.zeros((kept_total, count), jnp.int32)
    for c in range(kept_total):
        channels = jnp.where(row_ids == c, kept_ref[c], channels)
    turns = lax.rem(channels * positions, count)
    quarters = (turns + quarter // 2) // quarter
    rest = (turns - quarters * quarter).astype(jnp.float32) * (2.0 * math.pi / count)
    square = rest * rest
    sine = rest * (1 + square * (-1 / 6 + square * (1 / 120 + square * (-1 / 5040 + square * (1 / 362880)))))
    cosine = 1 + square * (-1 / 2 + square * (1 / 24 + square * (-1 / 720 + square * (1 / 40320))))
    odd = (quarters & 1) == 1
    cos_part = jnp.where(odd, sine, cosine)
    sin_part = jnp.where(odd, cosine, sine)
    cos_part = jnp.where(((quarters + 1) & 2) == 2, -cos_part, cos_part)
    sin_part = jnp.where((quarters & 2) == 2, -sin_part, sin_part)
    norm_scale = 1.0 / math.sqrt(count)
    table = jnp.concatenate([cos_part * norm_scale, -sin_part * norm_scale], axis=0)
    table = table.astype(jnp.bfloat16).astype(jnp.float32)
    for place, tap in enumerate(reversed(range(TAPS))):
        scaled = table * taps_ref[tap : tap + 1, :]
        high = scaled.astype(jnp.bfloat16).astype(jnp.float32)
        columns[place * rows : (place + 1) * rows, :] = high
        columns[(TAPS + place) * rows : (TAPS + place + 1) * rows, :] = scaled - high

    @pl.loop(0, count // LANES)
    def _(tile):
        part = pl.ds(pl.multiple_of(tile * LANES, LANES), LANES)
        wide[part, :] = columns[:, part].T.astype(jnp.bfloat16)


def spectra_kernel(
    kept_in, taps_in, samples_ref, history_ref, out_ref, held, columns, wide, sums, kept, taps, sems, past_sem, kept_sem, taps_sem
):
    frame_count, input_count, sample_count = samples_ref.shape
    kept_total = kept_in.shape[0]
    rows = 2 * kept_total
    lead = TAPS - 1
    total = frame_count // CHUNK
    first_block = lax.axis_index("vis") == 0

    def chunk_copy(index):
        first = (total - 1 - index) * CHUNK
        return pltpu.make_async_copy(
            samples_ref.at[pl.ds(first, CHUNK)], held.at[pl.ds(first + CHUNK, CHUNK)], sems.at[index]
        )

    past_copy = pltpu.make_async_copy(history_ref, held.at[pl.ds(CHUNK - lead, lead)], past_sem)
    kept_copy = pltpu.make_async_copy(kept_in, kept, kept_sem)
    taps_copy = pltpu.make_async_copy(taps_in, taps, taps_sem)
    kept_copy.start()
    taps_copy.start()
    chunk_copy(0).start()
    kept_copy.wait()
    taps_copy.wait()
    for index in range(1, WINDOW):
        chunk_copy(index).start()

    build_table(kept, taps, columns, wide)

    @pl.loop(0, sums.shape[1] // rows)
    def _(slot):
        for h in range(input_count // LANES):
            sums[h, pl.ds(pl.multiple_of(slot * rows, 8), rows), :] = jnp.zeros((rows, LANES), jnp.float32)

    @pl.loop(0, total + jnp.where(first_block, 1, 0))
    def _(index):
        @pl.when(index < total)
        def _():
            chunk_copy(index).wait()

        @pl.when(index + WINDOW < total)
        def _():
            chunk_copy(index + WINDOW).start()

        @pl.when((index + WINDOW == total) & first_block)
        def _():
            past_copy.start()

        @pl.when(index == total)
        def _():
            past_copy.wait()

        first = (total - index) * CHUNK
        block = held[pl.ds(first, CHUNK)].reshape(CHUNK * input_count, sample_count)
        products = jnp.dot(block, wide[...], preferred_element_type=jnp.float32)
        for k in range(CHUNK):
            turned = products[k * input_count : (k + 1) * input_count].T
            both = turned[: TAPS * rows] + turned[TAPS * rows :]
            place = pl.ds(pl.multiple_of((first + k) * rows, 8), TAPS * rows)
            for h in range(input_count // LANES):
                sums[h, place, :] = sums[h, place, :] + both[:, h * LANES : (h + 1) * LANES]

    halo_rows = lax.broadcasted_iota(jnp.int32, (8, LANES), 0)
    end = CHUNK + frame_count

    @pl.loop(0, kept_total)
    def _(c):
        for h in range(input_count // LANES):
            cols = slice(h * LANES, (h + 1) * LANES)
            for part in range(2):
                first = CHUNK * rows + part * kept_total + c
                column = sums[h, pl.ds(first, frame_count, stride=rows), :]
                out_ref[c, part * frame_count : (part + 1) * frame_count, cols] = column.astype(jnp.bfloat16)
            real_tail = sums[h, pl.ds(end * rows + c, 8, stride=rows), :]
            imag_tail = sums[h, pl.ds((end - lead) * rows + kept_total + c, 8, stride=rows), :]
            tail = jnp.where(halo_rows < lead, real_tail, jnp.where(halo_rows < 2 * lead, imag_tail, 0.0))
            out_ref[c, 2 * frame_count :, cols] = tail.astype(jnp.bfloat16)


def spectra_part(samples, history, fir_taps, kept_channels):
    frame_count, input_count, sample_count = samples.shape
    kept_total = kept_channels.shape[0]
    rows = 2 * kept_total
    wide_count = 2 * TAPS * rows
    return pl.pallas_call(
        spectra_kernel,
        out_shape=jax.ShapeDtypeStruct((kept_total, 2 * frame_count + 8, input_count), jnp.bfloat16),
        in_specs=[pl.BlockSpec(memory_space=pl.ANY)] * 4,
        out_specs=pl.BlockSpec(memory_space=pltpu.VMEM),
        scratch_shapes=[
            pltpu.VMEM((frame_count + CHUNK, input_count, sample_count), jnp.bfloat16),
            pltpu.VMEM((wide_count, sample_count), jnp.float32),
            pltpu.VMEM((sample_count, wide_count), jnp.bfloat16),
            pltpu.VMEM((input_count // LANES, (frame_count + CHUNK + 8) * rows, LANES), jnp.float32),
            pltpu.SMEM((kept_total,), jnp.int32),
            pltpu.VMEM((TAPS, sample_count), jnp.float32),
            pltpu.SemaphoreType.DMA((frame_count // CHUNK,)),
            pltpu.SemaphoreType.DMA,
            pltpu.SemaphoreType.DMA,
            pltpu.SemaphoreType.DMA,
        ],
        compiler_params=pltpu.CompilerParams(vmem_limit_bytes=62 * MIB),
    )(kept_channels, fir_taps, samples, history)


def correlate_kernel(own_ref, core_ref, chip_ref, far_ref, out_ref, pair, halos, *, frame_count, scale):
    step = pl.program_id(0)
    me = lax.axis_index("vis")
    sources, _, input_count = own_ref.shape
    input_total = sources * input_count
    lead = TAPS - 1
    row_count = out_ref.shape[1] * pl.num_programs(0)
    parts = (own_ref, core_ref, chip_ref, far_ref)

    @pl.when(step == 0)
    def _():
        for k, part in enumerate(parts):
            for s in range(sources):
                halos[me ^ k, :, s * input_count : (s + 1) * input_count] = part[s, 2 * frame_count :, :]
        halo_rows = lax.broadcasted_iota(jnp.int32, (8, input_total), 0)
        for k, part in enumerate(parts):
            block = me ^ k
            before = jnp.maximum(block - 1, 0)
            halo = halos[before].astype(jnp.float32)
            halo = jnp.where(block > 0, halo, 0.0)
            real_halo = jnp.where(halo_rows < lead, halo, 0.0)
            imag_halo = jnp.where(halo_rows < lead, pltpu.roll(halo, 8 - lead, 0), 0.0)
            for s in range(sources):
                cols = slice(s * input_count, (s + 1) * input_count)
                real = part[s, :frame_count, :].astype(jnp.float32)
                imag = part[s, frame_count : 2 * frame_count, :].astype(jnp.float32)
                real = jnp.concatenate([real[:8] + real_halo[:, cols], real[8:]], axis=0)
                imag = jnp.concatenate([imag[:8] + imag_halo[:, cols], imag[8:]], axis=0)
                base = k * 2 * frame_count
                pair[0, base : base + frame_count, cols] = real.astype(jnp.bfloat16)
                pair[0, base + frame_count : base + 2 * frame_count, cols] = imag.astype(jnp.bfloat16)
                pair[1, base : base + frame_count, cols] = (-imag).astype(jnp.bfloat16)
                pair[1, base + frame_count : base + 2 * frame_count, cols] = real.astype(jnp.bfloat16)

    first_row = pl.multiple_of(me * row_count + step * ROW_TILE, ROW_TILE)
    left = pair[0, :, pl.ds(first_row, ROW_TILE)].T

    def product(which, cols):
        return jnp.dot(left, pair[which, :, cols], preferred_element_type=jnp.float32) * scale

    for j in range(input_total // COL_TILE):
        cols = slice(j * COL_TILE, (j + 1) * COL_TILE)
        below = (j * COL_TILE < first_row).astype(jnp.int32)
        out_ref[0, :, cols] = product(below, cols).astype(jnp.bfloat16)

    corner = pl.multiple_of(first_row // COL_TILE * COL_TILE, COL_TILE)
    cols = pl.ds(corner, COL_TILE)
    row_ids = first_row + lax.broadcasted_iota(jnp.int32, (ROW_TILE, COL_TILE), 0)
    col_ids = corner + lax.broadcasted_iota(jnp.int32, (ROW_TILE, COL_TILE), 1)
    mixed = jnp.where(col_ids >= row_ids, product(0, cols), product(1, cols))
    out_ref[0, :, cols] = mixed.astype(jnp.bfloat16)


def correlate_part(parts, frame_count, row_count):
    sources, _, input_count = parts[0].shape
    input_total = sources * input_count
    block_total = len(parts)
    depth = 2 * frame_count * block_total
    return pl.pallas_call(
        lambda *refs: correlate_kernel(*refs, frame_count=frame_count, scale=1.0 / (frame_count * block_total)),
        grid=(row_count // ROW_TILE,),
        out_shape=jax.ShapeDtypeStruct((1, row_count, input_total), jnp.bfloat16),
        in_specs=[pl.BlockSpec(memory_space=pltpu.VMEM)] * block_total,
        out_specs=pl.BlockSpec((1, ROW_TILE, input_total), lambda g: (0, g, 0)),
        scratch_shapes=[
            pltpu.VMEM((2, depth, input_total), jnp.bfloat16),
            pltpu.VMEM((block_total, 8, input_total), jnp.bfloat16),
        ],
        compiler_params=pltpu.CompilerParams(vmem_limit_bytes=32 * MIB),
    )(*parts)


def exchanged(value, distance):
    count = lax.axis_size("vis")
    return lax.ppermute(value, "vis", [(source, source ^ distance) for source in range(count)])


def per_device(samples, history, fir_taps, kept_channels):
    vis_count = lax.axis_size("vis")
    inp_count = lax.axis_size("inp")
    frame_count, input_count, _ = samples.shape
    spectra = spectra_part(samples, history, fir_taps, kept_channels)
    own = lax.all_to_all(spectra, "inp", split_axis=0, concat_axis=0, tiled=True)
    chip = exchanged(own, 2)
    core = exchanged(own, 1)
    far = exchanged(chip, 1)
    return correlate_part((own, core, chip, far), frame_count, input_count * inp_count // vis_count)


def shifted(value, axis, steps):
    count = lax.axis_size(axis)
    initial, last = (max(0, -steps), min(count, count - steps))
    return lax.ppermute(value, axis, [(source, source + steps) for source in range(initial, last)])


def make_table(kept_channels, sample_count):
    positions = jnp.arange(sample_count, dtype=jnp.int32)
    products = kept_channels[:, None] * positions[None, :] % sample_count
    angles = products.astype(jnp.float32) * (2.0 * math.pi / sample_count)
    norm_scale = 1.0 / math.sqrt(sample_count)
    table = jnp.concatenate([jnp.cos(angles) * norm_scale, -jnp.sin(angles) * norm_scale], axis=0)
    return table.astype(jnp.bfloat16)


def per_device_plain(samples, history, fir_taps, kept_channels):
    vis_count = lax.axis_size("vis")
    vis_index = lax.axis_index("vis")
    inp_count = lax.axis_size("inp")
    frame_count, input_count, sample_count = samples.shape
    kept_total = kept_channels.shape[0]
    previous = shifted(samples[frame_count - TAPS + 1 :], "vis", 1)
    previous = jnp.where(vis_index == 0, history, previous)
    extended = jnp.concatenate([previous, samples], axis=0).astype(jnp.float32)
    weighted = fir_taps[0] * extended[0:frame_count]
    for tap in range(1, TAPS):
        weighted = weighted + fir_taps[tap] * extended[tap : tap + frame_count]
    spectra = jnp.einsum(
        "kn,fin->kfi",
        make_table(kept_channels, sample_count),
        weighted.astype(jnp.bfloat16),
        preferred_element_type=jnp.float32,
    ).astype(jnp.bfloat16)
    spectra = spectra.reshape(2, kept_total, frame_count, input_count)
    mine = lax.all_to_all(spectra, "inp", split_axis=1, concat_axis=3, tiled=True)
    mine = lax.all_gather(mine, "vis", axis=2, tiled=True)
    real, imag = mine[0], mine[1]
    stacked = jnp.concatenate([real, imag], axis=1)
    rotated = jnp.concatenate([-imag, real], axis=1)
    input_total = input_count * inp_count
    row_count = input_total // vis_count
    left = lax.dynamic_slice_in_dim(stacked, vis_index * row_count, row_count, 2)
    re_block = jnp.einsum("cfa,cfb->cab", left, stacked, preferred_element_type=jnp.float32)
    im_block = jnp.einsum("cfa,cfb->cab", left, rotated, preferred_element_type=jnp.float32)
    row_ids = vis_index * row_count + jnp.arange(row_count, dtype=jnp.int32)
    col_ids = jnp.arange(input_total, dtype=jnp.int32)
    packed = jnp.where(col_ids[None, None, :] >= row_ids[None, :, None], re_block, im_block)
    return (packed / float(frame_count * vis_count)).astype(jnp.bfloat16)


def solution(mesh):
    def run(samples, history, fir_taps, kept_channels):
        input_count = samples.shape[1] // mesh.shape["inp"]
        row_count = samples.shape[1] // mesh.shape["vis"]
        one_channel = kept_channels.shape[0] == mesh.shape["inp"]
        tiled = input_count % 128 == 0 and row_count % ROW_TILE == 0 and mesh.shape["vis"] == 4 and one_channel
        return jax.shard_map(
            per_device if tiled else per_device_plain,
            mesh=mesh,
            in_specs=(P("vis", "inp", None), P(None, "inp", None), P(), P()),
            out_specs=P("inp", "vis", None),
            check_vma=False,
        )(samples, history, fir_taps, kept_channels)

    return run
```

```python
import math

import jax
import jax.numpy as jnp
from jax import lax
from jax.experimental import pallas as pl
from jax.experimental.pallas import tpu as pltpu
from jax.sharding import PartitionSpec as P

TAPS = 4
CHUNK = 4
WINDOW = 3
PIPE = True
COL_TILE = 256
LANES = 128
MIB = 1024 * 1024


def build_table(kept_ref, taps_ref, columns, wide):
    kept_total = kept_ref.shape[0]
    rows = 2 * kept_total
    count = taps_ref.shape[1]
    quarter = count // 4
    row_ids = lax.broadcasted_iota(jnp.int32, (kept_total, count), 0)
    positions = lax.broadcasted_iota(jnp.int32, (kept_total, count), 1)
    channels = jnp.zeros((kept_total, count), jnp.int32)
    for c in range(kept_total):
        channels = jnp.where(row_ids == c, kept_ref[c], channels)
    turns = (channels * positions) & (count - 1)
    quarters = (turns + quarter // 2) >> (quarter.bit_length() - 1)
    rest = (turns - quarters * quarter).astype(jnp.float32) * (2.0 * math.pi / count)
    square = rest * rest
    sine = rest * (1 + square * (-1 / 6 + square * (1 / 120 + square * (-1 / 5040 + square * (1 / 362880)))))
    cosine = 1 + square * (-1 / 2 + square * (1 / 24 + square * (-1 / 720 + square * (1 / 40320))))
    odd = (quarters & 1) == 1
    cos_part = jnp.where(odd, sine, cosine)
    sin_part = jnp.where(odd, cosine, sine)
    cos_part = jnp.where(((quarters + 1) & 2) == 2, -cos_part, cos_part)
    sin_part = jnp.where((quarters & 2) == 2, -sin_part, sin_part)
    norm_scale = 1.0 / math.sqrt(count)
    table = jnp.concatenate([cos_part * norm_scale, -sin_part * norm_scale], axis=0)
    table = table.astype(jnp.bfloat16).astype(jnp.float32)
    for place, tap in enumerate(reversed(range(TAPS))):
        scaled = table * taps_ref[tap : tap + 1, :]
        high = scaled.astype(jnp.bfloat16).astype(jnp.float32)
        columns[place * rows : (place + 1) * rows, :] = high
        columns[(TAPS + place) * rows : (TAPS + place + 1) * rows, :] = scaled - high

    @pl.loop(0, count // LANES)
    def _(tile):
        part = pl.ds(pl.multiple_of(tile * LANES, LANES), LANES)
        wide[part, :] = columns[:, part].T.astype(jnp.bfloat16)


def spectra_kernel(
    kept_in, taps_in, samples_ref, history_ref, out_ref, held, columns, wide, sums, lines, products, kept, taps, sems, past_sem, kept_sem, taps_sem
):
    frame_count, input_count, sample_count = samples_ref.shape
    kept_total = kept_in.shape[0]
    rows = 2 * kept_total
    lead = TAPS - 1
    total = frame_count // CHUNK
    first_block = lax.axis_index("vis") == 0

    def chunk_copy(index):
        first = (total - 1 - index) * CHUNK
        return pltpu.make_async_copy(
            samples_ref.at[pl.ds(first, CHUNK)], held.at[pl.ds(first + CHUNK, CHUNK)], sems.at[index]
        )

    past_copy = pltpu.make_async_copy(history_ref, held.at[pl.ds(CHUNK - lead, lead)], past_sem)
    kept_copy = pltpu.make_async_copy(kept_in, kept, kept_sem)
    taps_copy = pltpu.make_async_copy(taps_in, taps, taps_sem)
    kept_copy.start()
    taps_copy.start()
    chunk_copy(0).start()
    kept_copy.wait()
    taps_copy.wait()
    for index in range(1, WINDOW):
        chunk_copy(index).start()

    build_table(kept, taps, columns, wide)

    @pl.loop(0, sums.shape[1] // rows)
    def _(slot):
        for h in range(input_count // LANES):
            sums[h, pl.ds(pl.multiple_of(slot * rows, 8), rows), :] = jnp.zeros((rows, LANES), jnp.float32)

    stride = lines.shape[1] // rows

    def add_chunk(first, values):
        for k in reversed(range(CHUNK)):
            turned = values[k * input_count : (k + 1) * input_count].T
            both = turned[: TAPS * rows] + turned[TAPS * rows :]
            place = pl.ds(pl.multiple_of((first + k) * rows, 8), TAPS * rows)
            for h in range(input_count // LANES):
                added = sums[h, place, :] + both[:, h * LANES : (h + 1) * LANES]
                sums[h, place, :] = added
                lines[h, pl.ds(first + k + lead + 8 - CHUNK, rows, stride=stride), :] = added[lead * rows :]

    if PIPE:
        products[...] = jnp.zeros_like(products)

    @pl.loop(0, total + jnp.where(first_block, 1, 0))
    def _(index):
        @pl.when(index < total)
        def _():
            chunk_copy(index).wait()

        @pl.when(index + WINDOW < total)
        def _():
            chunk_copy(index + WINDOW).start()

        @pl.when((index + WINDOW == total) & first_block)
        def _():
            past_copy.start()

        @pl.when(index == total)
        def _():
            past_copy.wait()

        first = (total - index) * CHUNK
        block = held[pl.ds(first, CHUNK)].reshape(CHUNK * input_count, sample_count)
        if PIPE:
            add_chunk(first + CHUNK, products[...])
            products[...] = jnp.dot(block, wide[...], preferred_element_type=jnp.float32)
        else:
            add_chunk(first, jnp.dot(block, wide[...], preferred_element_type=jnp.float32))

    if PIPE:
        add_chunk(jnp.where(first_block, 0, CHUNK), products[...])
    for slot in range(lead):
        for h in range(input_count // LANES):
            done = sums[h, (CHUNK + slot) * rows : (CHUNK + slot + 1) * rows, :]
            lines[h, pl.ds(8 + slot, rows, stride=stride), :] = done

    halo_rows = lax.broadcasted_iota(jnp.int32, (8, LANES), 0)
    for c in range(kept_total):
        for h in range(input_count // LANES):
            cols = slice(h * LANES, (h + 1) * LANES)
            for part in range(2):
                first = (part * kept_total + c) * stride + 8
                column = lines[h, first : first + frame_count, :]
                out_ref[c, part * frame_count : (part + 1) * frame_count, cols] = column.astype(jnp.bfloat16)
            first = c * stride + 8 + frame_count
            real_tail = lines[h, first : first + 8, :]
            first += kept_total * stride
            imag_tail = pltpu.roll(lines[h, first : first + 8, :], lead, 0)
            tail = jnp.where(halo_rows < lead, real_tail, jnp.where(halo_rows < 2 * lead, imag_tail, 0.0))
            out_ref[c, 2 * frame_count :, cols] = tail.astype(jnp.bfloat16)


def spectra_part(samples, history, fir_taps, kept_channels):
    frame_count, input_count, sample_count = samples.shape
    kept_total = kept_channels.shape[0]
    rows = 2 * kept_total
    wide_count = 2 * TAPS * rows
    return pl.pallas_call(
        spectra_kernel,
        out_shape=jax.ShapeDtypeStruct((kept_total, 2 * frame_count + 8, input_count), jnp.bfloat16),
        in_specs=[pl.BlockSpec(memory_space=pl.ANY)] * 4,
        out_specs=pl.BlockSpec(memory_space=pltpu.VMEM),
        scratch_shapes=[
            pltpu.VMEM((frame_count + CHUNK, input_count, sample_count), jnp.bfloat16),
            pltpu.VMEM((wide_count, sample_count), jnp.float32),
            pltpu.VMEM((sample_count, wide_count), jnp.bfloat16),
            pltpu.VMEM((input_count // LANES, (frame_count + CHUNK + 8) * rows, LANES), jnp.float32),
            pltpu.VMEM((input_count // LANES, rows * (frame_count + 16), LANES), jnp.float32),
            pltpu.VMEM((CHUNK * input_count, wide_count), jnp.float32),
            pltpu.SMEM((kept_total,), jnp.int32),
            pltpu.VMEM((TAPS, sample_count), jnp.float32),
            pltpu.SemaphoreType.DMA((frame_count // CHUNK,)),
            pltpu.SemaphoreType.DMA,
            pltpu.SemaphoreType.DMA,
            pltpu.SemaphoreType.DMA,
        ],
        compiler_params=pltpu.CompilerParams(vmem_limit_bytes=62 * MIB),
    )(kept_channels, fir_taps, samples, history)


def correlate_kernel(own_ref, core_ref, chip_ref, far_ref, out_ref, pair, halos, left, tiles, sems, *, frame_count, scale):
    me = lax.axis_index("vis")
    sources, _, input_count = own_ref.shape
    input_total = sources * input_count
    lead = TAPS - 1
    row_count = left.shape[1]
    parts = (own_ref, core_ref, chip_ref, far_ref)
    for k, part in enumerate(parts):
        for s in range(sources):
            halos[me ^ k, :, s * input_count : (s + 1) * input_count] = part[s, 2 * frame_count :, :]
    halo_rows = lax.broadcasted_iota(jnp.int32, (8, input_total), 0)
    rest = jnp.zeros((8, input_total), jnp.float32)
    for k, part in enumerate(parts):
        block = me ^ k
        halo = jnp.where(block > 0, halos[jnp.maximum(block - 1, 0)].astype(jnp.float32), 0.0)
        real_halo = jnp.concatenate([jnp.where(halo_rows < lead, halo, 0.0), rest], axis=0)
        imag_halo = jnp.concatenate([jnp.where(halo_rows < lead, pltpu.roll(halo, 8 - lead, 0), 0.0), rest], axis=0)
        for r, head in enumerate((real_halo, imag_halo)):
            base = (2 * k + r) * frame_count
            for s in range(sources):
                cols = slice(s * input_count, (s + 1) * input_count)
                first = part[s, r * frame_count : r * frame_count + 16, :].astype(jnp.float32) + head[:, cols]
                pair[base : base + 16, cols] = first.astype(jnp.bfloat16)
                pair[base + 16 : base + frame_count, cols] = part[s, r * frame_count + 16 : (r + 1) * frame_count, :]

    mine = pl.ds(pl.multiple_of(me * row_count, row_count), row_count)
    for k in range(len(parts)):
        base = 2 * k * frame_count
        real = pair[base : base + frame_count, mine].astype(jnp.float32) * scale
        imag = pair[base + frame_count : base + 2 * frame_count, mine].astype(jnp.float32) * scale
        left[0, :, base : base + 2 * frame_count] = jnp.concatenate([real, imag], axis=0).T.astype(jnp.bfloat16)
        left[1, :, base : base + 2 * frame_count] = jnp.concatenate([imag, -real], axis=0).T.astype(jnp.bfloat16)

    tile_total = input_total // COL_TILE
    corner_tiles = row_count // COL_TILE

    def tile_copy(t):
        place = lax.rem(me * corner_tiles + t, tile_total)
        cols = pl.ds(pl.multiple_of(place * COL_TILE, COL_TILE), COL_TILE)
        return pltpu.make_async_copy(tiles.at[t], out_ref.at[0, :, cols], sems.at[t])

    for t in range(tile_total):
        place = me * corner_tiles + t
        below = (place >= tile_total).astype(jnp.int32)
        place = lax.rem(place, tile_total)
        right = pair[:, pl.ds(pl.multiple_of(place * COL_TILE, COL_TILE), COL_TILE)]
        if t < corner_tiles:
            row_ids = lax.broadcasted_iota(jnp.int32, (row_count, COL_TILE), 0)
            col_ids = lax.broadcasted_iota(jnp.int32, (row_count, COL_TILE), 1) + t * COL_TILE
            real = jnp.dot(left[0], right, preferred_element_type=jnp.float32)
            imag = jnp.dot(left[1], right, preferred_element_type=jnp.float32)
            products = jnp.where(col_ids >= row_ids, real, imag)
        else:
            products = jnp.dot(left[below], right, preferred_element_type=jnp.float32)
        tiles[t] = products.astype(jnp.bfloat16)
        tile_copy(t).start()
    for t in range(tile_total):
        tile_copy(t).wait()


def correlate_part(parts, frame_count, row_count):
    sources, _, input_count = parts[0].shape
    input_total = sources * input_count
    block_total = len(parts)
    depth = 2 * frame_count * block_total
    tile_total = input_total // COL_TILE
    return pl.pallas_call(
        lambda *refs: correlate_kernel(*refs, frame_count=frame_count, scale=1.0 / (frame_count * block_total)),
        out_shape=jax.ShapeDtypeStruct((1, row_count, input_total), jnp.bfloat16),
        in_specs=[pl.BlockSpec(memory_space=pltpu.VMEM)] * block_total,
        out_specs=pl.BlockSpec(memory_space=pl.ANY),
        scratch_shapes=[
            pltpu.VMEM((depth, input_total), jnp.bfloat16),
            pltpu.VMEM((block_total, 8, input_total), jnp.bfloat16),
            pltpu.VMEM((2, row_count, depth), jnp.bfloat16),
            pltpu.VMEM((tile_total, row_count, COL_TILE), jnp.bfloat16),
            pltpu.SemaphoreType.DMA((tile_total,)),
        ],
        compiler_params=pltpu.CompilerParams(vmem_limit_bytes=32 * MIB),
    )(*parts)


def exchanged(value, distance):
    count = lax.axis_size("vis")
    return lax.ppermute(value, "vis", [(source, source ^ distance) for source in range(count)])


def per_device(samples, history, fir_taps, kept_channels):
    vis_count = lax.axis_size("vis")
    inp_count = lax.axis_size("inp")
    frame_count, input_count, _ = samples.shape
    spectra = spectra_part(samples, history, fir_taps, kept_channels)
    own = lax.all_to_all(spectra, "inp", split_axis=0, concat_axis=0, tiled=True)
    chip = exchanged(own, 2)
    core = exchanged(own, 1)
    far = exchanged(chip, 1)
    return correlate_part((own, core, chip, far), frame_count, input_count * inp_count // vis_count)


def shifted(value, axis, steps):
    count = lax.axis_size(axis)
    initial, last = (max(0, -steps), min(count, count - steps))
    return lax.ppermute(value, axis, [(source, source + steps) for source in range(initial, last)])


def make_table(kept_channels, sample_count):
    positions = jnp.arange(sample_count, dtype=jnp.int32)
    products = kept_channels[:, None] * positions[None, :] % sample_count
    angles = products.astype(jnp.float32) * (2.0 * math.pi / sample_count)
    norm_scale = 1.0 / math.sqrt(sample_count)
    table = jnp.concatenate([jnp.cos(angles) * norm_scale, -jnp.sin(angles) * norm_scale], axis=0)
    return table.astype(jnp.bfloat16)


def per_device_plain(samples, history, fir_taps, kept_channels):
    vis_count = lax.axis_size("vis")
    vis_index = lax.axis_index("vis")
    inp_count = lax.axis_size("inp")
    frame_count, input_count, sample_count = samples.shape
    kept_total = kept_channels.shape[0]
    previous = shifted(samples[frame_count - TAPS + 1 :], "vis", 1)
    previous = jnp.where(vis_index == 0, history, previous)
    extended = jnp.concatenate([previous, samples], axis=0).astype(jnp.float32)
    weighted = fir_taps[0] * extended[0:frame_count]
    for tap in range(1, TAPS):
        weighted = weighted + fir_taps[tap] * extended[tap : tap + frame_count]
    spectra = jnp.einsum(
        "kn,fin->kfi",
        make_table(kept_channels, sample_count),
        weighted.astype(jnp.bfloat16),
        preferred_element_type=jnp.float32,
    ).astype(jnp.bfloat16)
    spectra = spectra.reshape(2, kept_total, frame_count, input_count)
    mine = lax.all_to_all(spectra, "inp", split_axis=1, concat_axis=3, tiled=True)
    mine = lax.all_gather(mine, "vis", axis=2, tiled=True)
    real, imag = mine[0], mine[1]
    stacked = jnp.concatenate([real, imag], axis=1)
    rotated = jnp.concatenate([-imag, real], axis=1)
    input_total = input_count * inp_count
    row_count = input_total // vis_count
    left = lax.dynamic_slice_in_dim(stacked, vis_index * row_count, row_count, 2)
    re_block = jnp.einsum("cfa,cfb->cab", left, stacked, preferred_element_type=jnp.float32)
    im_block = jnp.einsum("cfa,cfb->cab", left, rotated, preferred_element_type=jnp.float32)
    row_ids = vis_index * row_count + jnp.arange(row_count, dtype=jnp.int32)
    col_ids = jnp.arange(input_total, dtype=jnp.int32)
    packed = jnp.where(col_ids[None, None, :] >= row_ids[None, :, None], re_block, im_block)
    return (packed / float(frame_count * vis_count)).astype(jnp.bfloat16)


def solution(mesh):
    def run(samples, history, fir_taps, kept_channels):
        input_count = samples.shape[1] // mesh.shape["inp"]
        row_count = samples.shape[1] // mesh.shape["vis"]
        one_channel = kept_channels.shape[0] == mesh.shape["inp"]
        frame_total, _, sample_total = samples.shape
        whole_tiles = input_count % LANES == 0 and row_count % COL_TILE == 0 and frame_total % 64 == 0
        binary = frame_total & (frame_total - 1) == 0 and sample_total & (sample_total - 1) == 0
        tiled = whole_tiles and binary and mesh.shape["vis"] == 4 and one_channel
        return jax.shard_map(
            per_device if tiled else per_device_plain,
            mesh=mesh,
            in_specs=(P("vis", "inp", None), P(None, "inp", None), P(), P()),
            out_specs=P("inp", "vis", None),
            check_vma=False,
        )(samples, history, fir_taps, kept_channels)

    return run
```

```python
import math

import jax
import jax.numpy as jnp
from jax import lax
from jax.experimental import pallas as pl
from jax.experimental.pallas import tpu as pltpu
from jax.sharding import PartitionSpec as P

TAPS = 4
CHUNK = 4
WINDOW = 3
COL_TILE = 256
LANES = 128
MIB = 1024 * 1024


def build_table(kept_ref, taps_ref, columns, wide):
    kept_total = kept_ref.shape[0]
    rows = 2 * kept_total
    count = taps_ref.shape[1]
    quarter = count // 4
    row_ids = lax.broadcasted_iota(jnp.int32, (kept_total, count), 0)
    positions = lax.broadcasted_iota(jnp.int32, (kept_total, count), 1)
    channels = jnp.zeros((kept_total, count), jnp.int32)
    for c in range(kept_total):
        channels = jnp.where(row_ids == c, kept_ref[c], channels)
    turns = (channels * positions) & (count - 1)
    quarters = (turns + quarter // 2) >> (quarter.bit_length() - 1)
    rest = (turns - quarters * quarter).astype(jnp.float32) * (2.0 * math.pi / count)
    square = rest * rest
    sine = rest * (1 + square * (-1 / 6 + square * (1 / 120 + square * (-1 / 5040 + square * (1 / 362880)))))
    cosine = 1 + square * (-1 / 2 + square * (1 / 24 + square * (-1 / 720 + square * (1 / 40320))))
    odd = (quarters & 1) == 1
    cos_part = jnp.where(odd, sine, cosine)
    sin_part = jnp.where(odd, cosine, sine)
    cos_part = jnp.where(((quarters + 1) & 2) == 2, -cos_part, cos_part)
    sin_part = jnp.where((quarters & 2) == 2, -sin_part, sin_part)
    norm_scale = 1.0 / math.sqrt(count)
    table = jnp.concatenate([cos_part * norm_scale, -sin_part * norm_scale], axis=0)
    table = table.astype(jnp.bfloat16).astype(jnp.float32)
    for place, tap in enumerate(reversed(range(TAPS))):
        scaled = table * taps_ref[tap : tap + 1, :]
        high = scaled.astype(jnp.bfloat16).astype(jnp.float32)
        columns[place * rows : (place + 1) * rows, :] = high
        columns[(TAPS + place) * rows : (TAPS + place + 1) * rows, :] = scaled - high

    for tile in range(count // LANES):
        part = slice(tile * LANES, (tile + 1) * LANES)
        wide[part, :] = columns[:, part].T.astype(jnp.bfloat16)


def spectra_kernel(
    kept_in, taps_in, samples_ref, history_ref, out_ref, held, columns, wide, sums, lines, products, kept, taps, sems, past_sem, kept_sem, taps_sem
):
    frame_count, input_count, sample_count = samples_ref.shape
    kept_total = kept_in.shape[0]
    rows = 2 * kept_total
    lead = TAPS - 1
    total = frame_count // CHUNK
    first_block = lax.axis_index("vis") == 0

    def chunk_copy(index):
        first = (total - 1 - index) * CHUNK
        return pltpu.make_async_copy(
            samples_ref.at[pl.ds(first, CHUNK)], held.at[pl.ds(first + CHUNK, CHUNK)], sems.at[index]
        )

    past_copy = pltpu.make_async_copy(history_ref, held.at[pl.ds(CHUNK - lead, lead)], past_sem)
    kept_copy = pltpu.make_async_copy(kept_in, kept, kept_sem)
    taps_copy = pltpu.make_async_copy(taps_in, taps, taps_sem)
    kept_copy.start()
    taps_copy.start()
    chunk_copy(0).start()
    products[...] = jnp.zeros_like(products)
    sums[...] = jnp.zeros_like(sums)
    kept_copy.wait()
    taps_copy.wait()
    for index in range(1, WINDOW):
        chunk_copy(index).start()

    build_table(kept, taps, columns, wide)

    stride = lines.shape[1] // rows

    def add_chunk(first, values):
        for k in reversed(range(CHUNK)):
            turned = values[k * input_count : (k + 1) * input_count].T
            both = turned[: TAPS * rows] + turned[TAPS * rows :]
            place = pl.ds(pl.multiple_of((first + k) * rows, 8), TAPS * rows)
            for h in range(input_count // LANES):
                added = sums[h, place, :] + both[:, h * LANES : (h + 1) * LANES]
                sums[h, place, :] = added
                lines[h, pl.ds(first + k + lead + 8 - CHUNK, rows, stride=stride), :] = added[lead * rows :]

    @pl.loop(0, total + jnp.where(first_block, 1, 0))
    def _(index):
        @pl.when(index < total)
        def _():
            chunk_copy(index).wait()

        @pl.when(index + WINDOW < total)
        def _():
            chunk_copy(index + WINDOW).start()

        @pl.when((index + WINDOW == total) & first_block)
        def _():
            past_copy.start()

        @pl.when(index == total)
        def _():
            past_copy.wait()

        first = (total - index) * CHUNK
        block = held[pl.ds(first, CHUNK)].reshape(CHUNK * input_count, sample_count)
        add_chunk(first + CHUNK, products[...])
        products[...] = jnp.dot(block, wide[...], preferred_element_type=jnp.float32)

    add_chunk(jnp.where(first_block, 0, CHUNK), products[...])
    for slot in range(lead):
        for h in range(input_count // LANES):
            done = sums[h, (CHUNK + slot) * rows : (CHUNK + slot + 1) * rows, :]
            lines[h, pl.ds(8 + slot, rows, stride=stride), :] = done

    halo_rows = lax.broadcasted_iota(jnp.int32, (8, LANES), 0)
    for c in range(kept_total):
        for h in range(input_count // LANES):
            cols = slice(h * LANES, (h + 1) * LANES)
            for part in range(2):
                first = (part * kept_total + c) * stride + 8
                column = lines[h, first : first + frame_count, :]
                out_ref[c, part * frame_count : (part + 1) * frame_count, cols] = column.astype(jnp.bfloat16)
            first = c * stride + 8 + frame_count
            real_tail = lines[h, first : first + 8, :]
            first += kept_total * stride
            imag_tail = pltpu.roll(lines[h, first : first + 8, :], lead, 0)
            tail = jnp.where(halo_rows < lead, real_tail, jnp.where(halo_rows < 2 * lead, imag_tail, 0.0))
            out_ref[c, 2 * frame_count :, cols] = tail.astype(jnp.bfloat16)


def spectra_part(samples, history, fir_taps, kept_channels):
    frame_count, input_count, sample_count = samples.shape
    kept_total = kept_channels.shape[0]
    rows = 2 * kept_total
    wide_count = 2 * TAPS * rows
    return pl.pallas_call(
        spectra_kernel,
        out_shape=jax.ShapeDtypeStruct((kept_total, 2 * frame_count + 8, input_count), jnp.bfloat16),
        in_specs=[pl.BlockSpec(memory_space=pl.ANY)] * 4,
        out_specs=pl.BlockSpec(memory_space=pltpu.VMEM),
        scratch_shapes=[
            pltpu.VMEM((frame_count + CHUNK, input_count, sample_count), jnp.bfloat16),
            pltpu.VMEM((wide_count, sample_count), jnp.float32),
            pltpu.VMEM((sample_count, wide_count), jnp.bfloat16),
            pltpu.VMEM((input_count // LANES, (frame_count + CHUNK + 8) * rows, LANES), jnp.float32),
            pltpu.VMEM((input_count // LANES, rows * (frame_count + 16), LANES), jnp.float32),
            pltpu.VMEM((CHUNK * input_count, wide_count), jnp.float32),
            pltpu.SMEM((kept_total,), jnp.int32),
            pltpu.VMEM((TAPS, sample_count), jnp.float32),
            pltpu.SemaphoreType.DMA((frame_count // CHUNK,)),
            pltpu.SemaphoreType.DMA,
            pltpu.SemaphoreType.DMA,
            pltpu.SemaphoreType.DMA,
        ],
        compiler_params=pltpu.CompilerParams(vmem_limit_bytes=62 * MIB),
    )(kept_channels, fir_taps, samples, history)


def correlate_kernel(own_ref, core_ref, chip_ref, far_ref, out_ref, pair, halos, left, tiles, sems, *, frame_count, scale):
    me = lax.axis_index("vis")
    sources, _, input_count = own_ref.shape
    input_total = sources * input_count
    lead = TAPS - 1
    row_count = left.shape[1]
    parts = (own_ref, core_ref, chip_ref, far_ref)
    for k, part in enumerate(parts):
        for s in range(sources):
            halos[me ^ k, :, s * input_count : (s + 1) * input_count] = part[s, 2 * frame_count :, :]
    halo_rows = lax.broadcasted_iota(jnp.int32, (8, input_total), 0)
    rest = jnp.zeros((8, input_total), jnp.float32)
    for k, part in enumerate(parts):
        block = me ^ k
        halo = jnp.where(block > 0, halos[jnp.maximum(block - 1, 0)].astype(jnp.float32), 0.0)
        real_halo = jnp.concatenate([jnp.where(halo_rows < lead, halo, 0.0), rest], axis=0)
        imag_halo = jnp.concatenate([jnp.where(halo_rows < lead, pltpu.roll(halo, 8 - lead, 0), 0.0), rest], axis=0)
        for r, head in enumerate((real_halo, imag_halo)):
            base = (r * len(parts) + k) * frame_count
            for s in range(sources):
                cols = slice(s * input_count, (s + 1) * input_count)
                first = part[s, r * frame_count : r * frame_count + 16, :].astype(jnp.float32) + head[:, cols]
                pair[base : base + 16, cols] = first.astype(jnp.bfloat16)
                pair[base + 16 : base + frame_count, cols] = part[s, r * frame_count + 16 : (r + 1) * frame_count, :]

    mine = pl.ds(pl.multiple_of(me * row_count, row_count), row_count)
    half = frame_count * len(parts)
    real = pair[:half, mine].T * scale
    imag = pair[half:, mine].T * scale
    left[0, :, :half] = real
    left[0, :, half:] = imag
    left[1, :, :half] = imag
    left[1, :, half:] = -real

    tile_total = input_total // COL_TILE
    corner_tiles = row_count // COL_TILE

    def tile_copy(t):
        place = lax.rem(me * corner_tiles + t, tile_total)
        cols = pl.ds(pl.multiple_of(place * COL_TILE, COL_TILE), COL_TILE)
        return pltpu.make_async_copy(tiles.at[t], out_ref.at[0, :, cols], sems.at[t])

    for t in range(tile_total):
        place = me * corner_tiles + t
        below = (place >= tile_total).astype(jnp.int32)
        place = lax.rem(place, tile_total)
        right = pair[:, pl.ds(pl.multiple_of(place * COL_TILE, COL_TILE), COL_TILE)]
        if t < corner_tiles:
            row_ids = lax.broadcasted_iota(jnp.int32, (row_count, COL_TILE), 0)
            col_ids = lax.broadcasted_iota(jnp.int32, (row_count, COL_TILE), 1) + t * COL_TILE
            real = jnp.dot(left[0], right, preferred_element_type=jnp.float32)
            imag = jnp.dot(left[1], right, preferred_element_type=jnp.float32)
            products = jnp.where(col_ids >= row_ids, real, imag)
        else:
            products = jnp.dot(left[below], right, preferred_element_type=jnp.float32)
        tiles[t] = products.astype(jnp.bfloat16)
        tile_copy(t).start()
    for t in range(tile_total):
        tile_copy(t).wait()


def correlate_part(parts, frame_count, row_count):
    sources, _, input_count = parts[0].shape
    input_total = sources * input_count
    block_total = len(parts)
    depth = 2 * frame_count * block_total
    tile_total = input_total // COL_TILE
    return pl.pallas_call(
        lambda *refs: correlate_kernel(*refs, frame_count=frame_count, scale=jnp.bfloat16(1.0 / (frame_count * block_total))),
        out_shape=jax.ShapeDtypeStruct((1, row_count, input_total), jnp.bfloat16),
        in_specs=[pl.BlockSpec(memory_space=pltpu.VMEM)] * block_total,
        out_specs=pl.BlockSpec(memory_space=pl.ANY),
        scratch_shapes=[
            pltpu.VMEM((depth, input_total), jnp.bfloat16),
            pltpu.VMEM((block_total, 8, input_total), jnp.bfloat16),
            pltpu.VMEM((2, row_count, depth), jnp.bfloat16),
            pltpu.VMEM((tile_total, row_count, COL_TILE), jnp.bfloat16),
            pltpu.SemaphoreType.DMA((tile_total,)),
        ],
        compiler_params=pltpu.CompilerParams(vmem_limit_bytes=32 * MIB),
    )(*parts)


def exchanged(value, distance):
    count = lax.axis_size("vis")
    return lax.ppermute(value, "vis", [(source, source ^ distance) for source in range(count)])


def per_device(samples, history, fir_taps, kept_channels):
    vis_count = lax.axis_size("vis")
    inp_count = lax.axis_size("inp")
    frame_count, input_count, _ = samples.shape
    spectra = spectra_part(samples, history, fir_taps, kept_channels)
    own = lax.all_to_all(spectra, "inp", split_axis=0, concat_axis=0, tiled=True)
    chip = exchanged(own, 2)
    core = exchanged(own, 1)
    far = exchanged(chip, 1)
    return correlate_part((own, core, chip, far), frame_count, input_count * inp_count // vis_count)


def shifted(value, axis, steps):
    count = lax.axis_size(axis)
    initial, last = (max(0, -steps), min(count, count - steps))
    return lax.ppermute(value, axis, [(source, source + steps) for source in range(initial, last)])


def make_table(kept_channels, sample_count):
    positions = jnp.arange(sample_count, dtype=jnp.int32)
    products = kept_channels[:, None] * positions[None, :] % sample_count
    angles = products.astype(jnp.float32) * (2.0 * math.pi / sample_count)
    norm_scale = 1.0 / math.sqrt(sample_count)
    table = jnp.concatenate([jnp.cos(angles) * norm_scale, -jnp.sin(angles) * norm_scale], axis=0)
    return table.astype(jnp.bfloat16)


def per_device_plain(samples, history, fir_taps, kept_channels):
    vis_count = lax.axis_size("vis")
    vis_index = lax.axis_index("vis")
    inp_count = lax.axis_size("inp")
    frame_count, input_count, sample_count = samples.shape
    kept_total = kept_channels.shape[0]
    previous = shifted(samples[frame_count - TAPS + 1 :], "vis", 1)
    previous = jnp.where(vis_index == 0, history, previous)
    extended = jnp.concatenate([previous, samples], axis=0).astype(jnp.float32)
    weighted = fir_taps[0] * extended[0:frame_count]
    for tap in range(1, TAPS):
        weighted = weighted + fir_taps[tap] * extended[tap : tap + frame_count]
    spectra = jnp.einsum(
        "kn,fin->kfi",
        make_table(kept_channels, sample_count),
        weighted.astype(jnp.bfloat16),
        preferred_element_type=jnp.float32,
    ).astype(jnp.bfloat16)
    spectra = spectra.reshape(2, kept_total, frame_count, input_count)
    mine = lax.all_to_all(spectra, "inp", split_axis=1, concat_axis=3, tiled=True)
    mine = lax.all_gather(mine, "vis", axis=2, tiled=True)
    real, imag = mine[0], mine[1]
    stacked = jnp.concatenate([real, imag], axis=1)
    rotated = jnp.concatenate([-imag, real], axis=1)
    input_total = input_count * inp_count
    row_count = input_total // vis_count
    left = lax.dynamic_slice_in_dim(stacked, vis_index * row_count, row_count, 2)
    re_block = jnp.einsum("cfa,cfb->cab", left, stacked, preferred_element_type=jnp.float32)
    im_block = jnp.einsum("cfa,cfb->cab", left, rotated, preferred_element_type=jnp.float32)
    row_ids = vis_index * row_count + jnp.arange(row_count, dtype=jnp.int32)
    col_ids = jnp.arange(input_total, dtype=jnp.int32)
    packed = jnp.where(col_ids[None, None, :] >= row_ids[None, :, None], re_block, im_block)
    return (packed / float(frame_count * vis_count)).astype(jnp.bfloat16)


def solution(mesh):
    def run(samples, history, fir_taps, kept_channels):
        input_count = samples.shape[1] // mesh.shape["inp"]
        row_count = samples.shape[1] // mesh.shape["vis"]
        one_channel = kept_channels.shape[0] == mesh.shape["inp"]
        frame_total, _, sample_total = samples.shape
        whole_tiles = input_count % LANES == 0 and row_count % COL_TILE == 0 and frame_total % 64 == 0
        binary = frame_total & (frame_total - 1) == 0 and sample_total & (sample_total - 1) == 0
        tiled = whole_tiles and binary and mesh.shape["vis"] == 4 and one_channel
        return jax.shard_map(
            per_device if tiled else per_device_plain,
            mesh=mesh,
            in_specs=(P("vis", "inp", None), P(None, "inp", None), P(), P()),
            out_specs=P("inp", "vis", None),
            check_vma=False,
        )(samples, history, fir_taps, kept_channels)

    return run
```

```python
import math

import jax
import jax.numpy as jnp
from jax import lax
from jax.experimental import pallas as pl
from jax.experimental.pallas import tpu as pltpu
from jax.sharding import PartitionSpec as P

TAPS = 4
CHUNK = 4
WINDOW = 3
COL_TILE = 256
LANES = 128
MIB = 1024 * 1024


def build_table(kept_ref, taps_ref, columns, wide):
    kept_total = kept_ref.shape[0]
    rows = 2 * kept_total
    count = taps_ref.shape[1]
    quarter = count // 4
    row_ids = lax.broadcasted_iota(jnp.int32, (kept_total, count), 0)
    positions = lax.broadcasted_iota(jnp.int32, (kept_total, count), 1)
    channels = jnp.zeros((kept_total, count), jnp.int32)
    for c in range(kept_total):
        channels = jnp.where(row_ids == c, kept_ref[c], channels)
    turns = (channels * positions) & (count - 1)
    quarters = (turns + quarter // 2) >> (quarter.bit_length() - 1)
    rest = (turns - quarters * quarter).astype(jnp.float32) * (2.0 * math.pi / count)
    square = rest * rest
    sine = rest * (1 + square * (-1 / 6 + square * (1 / 120 + square * (-1 / 5040 + square * (1 / 362880)))))
    cosine = 1 + square * (-1 / 2 + square * (1 / 24 + square * (-1 / 720 + square * (1 / 40320))))
    odd = (quarters & 1) == 1
    cos_part = jnp.where(odd, sine, cosine)
    sin_part = jnp.where(odd, cosine, sine)
    cos_part = jnp.where(((quarters + 1) & 2) == 2, -cos_part, cos_part)
    sin_part = jnp.where((quarters & 2) == 2, -sin_part, sin_part)
    norm_scale = 1.0 / math.sqrt(count)
    table = jnp.concatenate([cos_part * norm_scale, -sin_part * norm_scale], axis=0)
    table = table.astype(jnp.bfloat16).astype(jnp.float32)
    for place, tap in enumerate(reversed(range(TAPS))):
        scaled = table * taps_ref[tap : tap + 1, :]
        high = scaled.astype(jnp.bfloat16).astype(jnp.float32)
        columns[place * rows : (place + 1) * rows, :] = high
        columns[(TAPS + place) * rows : (TAPS + place + 1) * rows, :] = scaled - high

    for tile in range(count // LANES):
        part = slice(tile * LANES, (tile + 1) * LANES)
        wide[part, :] = columns[:, part].T.astype(jnp.bfloat16)


def spectra_kernel(
    kept_in, taps_in, samples_ref, history_ref, out_ref,
    held, past, columns, wide, sums, lines, products, earlier, kept, taps, sems, past_sem, kept_sem, taps_sem,
):
    frame_count, input_count, sample_count = samples_ref.shape
    kept_total = kept_in.shape[0]
    rows = 2 * kept_total
    lead = TAPS - 1
    total = frame_count // CHUNK
    block = lax.axis_index("vis")
    mine = jnp.where(block == 0, 1, jnp.where(block == 3, 2, 0))

    def chunk_copy(index):
        part = pl.ds((total - 1 - index) * CHUNK, CHUNK)
        return pltpu.make_async_copy(samples_ref.at[part], held.at[part], sems.at[index])

    past_copy = pltpu.make_async_copy(history_ref.at[mine], past, past_sem)
    kept_copy = pltpu.make_async_copy(kept_in, kept, kept_sem)
    taps_copy = pltpu.make_async_copy(taps_in, taps, taps_sem)
    kept_copy.start()
    taps_copy.start()
    past_copy.start()
    chunk_copy(0).start()
    products[...] = jnp.zeros_like(products)
    sums[...] = jnp.zeros_like(sums)
    kept_copy.wait()
    taps_copy.wait()
    for index in range(1, WINDOW):
        chunk_copy(index).start()

    build_table(kept, taps, columns, wide)

    def tap_rows(values):
        turned = values.T
        return turned[: TAPS * rows] + turned[TAPS * rows :]

    def add_rows(slot, both, h):
        place = pl.ds(pl.multiple_of(slot * rows, 8), TAPS * rows)
        added = sums[h, place, :] + both[:, h * LANES : (h + 1) * LANES]
        sums[h, place, :] = added
        return added

    stride = lines.shape[1] // rows

    def add_chunk(first, values):
        for k in reversed(range(CHUNK)):
            both = tap_rows(values[k * input_count : (k + 1) * input_count])
            for h in range(input_count // LANES):
                added = add_rows(first + k + CHUNK, both, h)
                lines[h, pl.ds(first + k + lead + 8, rows, stride=stride), :] = added[lead * rows :]

    past_copy.wait()
    earlier[...] = tap_rows(jnp.dot(past[...], wide[...], preferred_element_type=jnp.float32))

    @pl.when(block == 0)
    def _():
        for h in range(input_count // LANES):
            add_rows(CHUNK - 2, earlier[...], h)

    @pl.loop(0, total)
    def _(index):
        chunk_copy(index).wait()

        @pl.when(index + WINDOW < total)
        def _():
            chunk_copy(index + WINDOW).start()

        first = (total - 1 - index) * CHUNK
        chunk = held[pl.ds(first, CHUNK)].reshape(CHUNK * input_count, sample_count)
        add_chunk(first + CHUNK, products[...])
        products[...] = jnp.dot(chunk, wide[...], preferred_element_type=jnp.float32)

    add_chunk(0, products[...])
    end = 8 + frame_count
    for h in range(input_count // LANES):
        cols = slice(h * LANES, (h + 1) * LANES)
        for frame in range(lead):
            done = sums[h, (CHUNK + frame) * rows : (CHUNK + frame + 1) * rows, :]
            lines[h, pl.ds(8 + frame, rows, stride=stride), :] = done
        lines[h, pl.ds(end + lead, rows, stride=stride), :] = earlier[lead * rows :, cols]

    @pl.when(block == 3)
    def _():
        for h in range(input_count // LANES):
            cols = slice(h * LANES, (h + 1) * LANES)
            for frame in range(lead):
                part = slice((frame + 1) * rows, (frame + 2) * rows)
                lines[h, pl.ds(end + frame, rows, stride=stride), :] = earlier[part, cols]

    place = lax.broadcasted_iota(jnp.int32, (8, LANES), 0)
    for c in range(kept_total):
        for h in range(input_count // LANES):
            cols = slice(h * LANES, (h + 1) * LANES)
            for part in range(2):
                first = (part * kept_total + c) * stride + 8
                column = lines[h, first : first + frame_count, :]
                out_ref[c, part * frame_count : (part + 1) * frame_count, cols] = column.astype(jnp.bfloat16)
            real = lines[h, c * stride + end : c * stride + end + 8, :]
            imag = lines[h, (kept_total + c) * stride + end : (kept_total + c) * stride + end + 8, :]
            spare = jnp.where(place == 2 * lead, pltpu.roll(real, lead, 0), pltpu.roll(imag, lead + 1, 0))
            tail = jnp.where(place < lead, real, jnp.where(place < 2 * lead, pltpu.roll(imag, lead, 0), spare))
            out_ref[c, 2 * frame_count :, cols] = tail.astype(jnp.bfloat16)


def spectra_part(samples, history, fir_taps, kept_channels):
    frame_count, input_count, sample_count = samples.shape
    kept_total = kept_channels.shape[0]
    rows = 2 * kept_total
    wide_count = 2 * TAPS * rows
    return pl.pallas_call(
        spectra_kernel,
        out_shape=jax.ShapeDtypeStruct((kept_total, 2 * frame_count + 8, input_count), jnp.bfloat16),
        in_specs=[pl.BlockSpec(memory_space=pl.ANY)] * 4,
        out_specs=pl.BlockSpec(memory_space=pltpu.VMEM),
        scratch_shapes=[
            pltpu.VMEM((frame_count, input_count, sample_count), jnp.bfloat16),
            pltpu.VMEM((input_count, sample_count), jnp.bfloat16),
            pltpu.VMEM((wide_count, sample_count), jnp.float32),
            pltpu.VMEM((sample_count, wide_count), jnp.bfloat16),
            pltpu.VMEM((input_count // LANES, (frame_count + CHUNK + 8) * rows, LANES), jnp.float32),
            pltpu.VMEM((input_count // LANES, rows * (frame_count + 16), LANES), jnp.float32),
            pltpu.VMEM((CHUNK * input_count, wide_count), jnp.float32),
            pltpu.VMEM((TAPS * rows, input_count), jnp.float32),
            pltpu.SMEM((kept_total,), jnp.int32),
            pltpu.VMEM((TAPS, sample_count), jnp.float32),
            pltpu.SemaphoreType.DMA((frame_count // CHUNK,)),
            pltpu.SemaphoreType.DMA,
            pltpu.SemaphoreType.DMA,
            pltpu.SemaphoreType.DMA,
        ],
        compiler_params=pltpu.CompilerParams(vmem_limit_bytes=62 * MIB),
    )(kept_channels, fir_taps, samples, history)


def correlate_kernel(own_ref, core_ref, chip_ref, far_ref, out_ref, pair, halos, left, tiles, sems, *, frame_count, scale):
    me = lax.axis_index("vis")
    sources, _, input_count = own_ref.shape
    input_total = sources * input_count
    lead = TAPS - 1
    row_count = left.shape[1]
    parts = (own_ref, core_ref, chip_ref, far_ref)
    for k, part in enumerate(parts):
        for s in range(sources):
            halos[me ^ k, :, s * input_count : (s + 1) * input_count] = part[s, 2 * frame_count :, :]
    halo_rows = lax.broadcasted_iota(jnp.int32, (8, input_total), 0)
    rest = jnp.zeros((8, input_total), jnp.float32)
    oldest = halos[len(parts) - 2].astype(jnp.float32)
    for k, part in enumerate(parts):
        block = me ^ k
        halo = halos[lax.rem(block + len(parts) - 1, len(parts))].astype(jnp.float32)
        spare = (halo_rows == 0) & (block == 0)
        real_halo = jnp.where(halo_rows < lead, halo, 0.0) + jnp.where(spare, pltpu.roll(oldest, 2, 0), 0.0)
        imag_halo = jnp.where(halo_rows < lead, pltpu.roll(halo, 8 - lead, 0), 0.0) + jnp.where(spare, pltpu.roll(oldest, 1, 0), 0.0)
        real_halo = jnp.concatenate([real_halo, rest], axis=0)
        imag_halo = jnp.concatenate([imag_halo, rest], axis=0)
        for r, head in enumerate((real_halo, imag_halo)):
            base = (r * len(parts) + k) * frame_count
            for s in range(sources):
                cols = slice(s * input_count, (s + 1) * input_count)
                first = part[s, r * frame_count : r * frame_count + 16, :].astype(jnp.float32) + head[:, cols]
                pair[base : base + 16, cols] = first.astype(jnp.bfloat16)
                pair[base + 16 : base + frame_count, cols] = part[s, r * frame_count + 16 : (r + 1) * frame_count, :]

    mine = pl.ds(pl.multiple_of(me * row_count, row_count), row_count)
    half = frame_count * len(parts)
    real = pair[:half, mine].T * scale
    imag = pair[half:, mine].T * scale
    left[0, :, :half] = real
    left[0, :, half:] = imag
    left[1, :, :half] = imag
    left[1, :, half:] = -real

    tile_total = input_total // COL_TILE
    corner_tiles = row_count // COL_TILE

    def tile_copy(t):
        place = lax.rem(me * corner_tiles + t, tile_total)
        cols = pl.ds(pl.multiple_of(place * COL_TILE, COL_TILE), COL_TILE)
        return pltpu.make_async_copy(tiles.at[t], out_ref.at[0, :, cols], sems.at[t])

    for t in range(tile_total):
        place = me * corner_tiles + t
        below = (place >= tile_total).astype(jnp.int32)
        place = lax.rem(place, tile_total)
        right = pair[:, pl.ds(pl.multiple_of(place * COL_TILE, COL_TILE), COL_TILE)]
        if t < corner_tiles:
            row_ids = lax.broadcasted_iota(jnp.int32, (row_count, COL_TILE), 0)
            col_ids = lax.broadcasted_iota(jnp.int32, (row_count, COL_TILE), 1) + t * COL_TILE
            real = jnp.dot(left[0], right, preferred_element_type=jnp.float32)
            imag = jnp.dot(left[1], right, preferred_element_type=jnp.float32)
            products = jnp.where(col_ids >= row_ids, real, imag)
        else:
            products = jnp.dot(left[below], right, preferred_element_type=jnp.float32)
        tiles[t] = products.astype(jnp.bfloat16)
        tile_copy(t).start()
    for t in range(tile_total):
        tile_copy(t).wait()


def correlate_part(parts, frame_count, row_count):
    sources, _, input_count = parts[0].shape
    input_total = sources * input_count
    block_total = len(parts)
    depth = 2 * frame_count * block_total
    tile_total = input_total // COL_TILE
    return pl.pallas_call(
        lambda *refs: correlate_kernel(*refs, frame_count=frame_count, scale=jnp.bfloat16(1.0 / (frame_count * block_total))),
        out_shape=jax.ShapeDtypeStruct((1, row_count, input_total), jnp.bfloat16),
        in_specs=[pl.BlockSpec(memory_space=pltpu.VMEM)] * block_total,
        out_specs=pl.BlockSpec(memory_space=pl.ANY),
        scratch_shapes=[
            pltpu.VMEM((depth, input_total), jnp.bfloat16),
            pltpu.VMEM((block_total, 8, input_total), jnp.bfloat16),
            pltpu.VMEM((2, row_count, depth), jnp.bfloat16),
            pltpu.VMEM((tile_total, row_count, COL_TILE), jnp.bfloat16),
            pltpu.SemaphoreType.DMA((tile_total,)),
        ],
        compiler_params=pltpu.CompilerParams(vmem_limit_bytes=32 * MIB),
    )(*parts)


def exchanged(value, distance):
    count = lax.axis_size("vis")
    return lax.ppermute(value, "vis", [(source, source ^ distance) for source in range(count)])


def per_device(samples, history, fir_taps, kept_channels):
    vis_count = lax.axis_size("vis")
    inp_count = lax.axis_size("inp")
    frame_count, input_count, _ = samples.shape
    spectra = spectra_part(samples, history, fir_taps, kept_channels)
    own = lax.all_to_all(spectra, "inp", split_axis=0, concat_axis=0, tiled=True)
    chip = exchanged(own, 2)
    core = exchanged(own, 1)
    far = exchanged(chip, 1)
    return correlate_part((own, core, chip, far), frame_count, input_count * inp_count // vis_count)


def shifted(value, axis, steps):
    count = lax.axis_size(axis)
    initial, last = (max(0, -steps), min(count, count - steps))
    return lax.ppermute(value, axis, [(source, source + steps) for source in range(initial, last)])


def make_table(kept_channels, sample_count):
    positions = jnp.arange(sample_count, dtype=jnp.int32)
    products = kept_channels[:, None] * positions[None, :] % sample_count
    angles = products.astype(jnp.float32) * (2.0 * math.pi / sample_count)
    norm_scale = 1.0 / math.sqrt(sample_count)
    table = jnp.concatenate([jnp.cos(angles) * norm_scale, -jnp.sin(angles) * norm_scale], axis=0)
    return table.astype(jnp.bfloat16)


def per_device_plain(samples, history, fir_taps, kept_channels):
    vis_count = lax.axis_size("vis")
    vis_index = lax.axis_index("vis")
    inp_count = lax.axis_size("inp")
    frame_count, input_count, sample_count = samples.shape
    kept_total = kept_channels.shape[0]
    previous = shifted(samples[frame_count - TAPS + 1 :], "vis", 1)
    previous = jnp.where(vis_index == 0, history, previous)
    extended = jnp.concatenate([previous, samples], axis=0).astype(jnp.float32)
    weighted = fir_taps[0] * extended[0:frame_count]
    for tap in range(1, TAPS):
        weighted = weighted + fir_taps[tap] * extended[tap : tap + frame_count]
    spectra = jnp.einsum(
        "kn,fin->kfi",
        make_table(kept_channels, sample_count),
        weighted.astype(jnp.bfloat16),
        preferred_element_type=jnp.float32,
    ).astype(jnp.bfloat16)
    spectra = spectra.reshape(2, kept_total, frame_count, input_count)
    mine = lax.all_to_all(spectra, "inp", split_axis=1, concat_axis=3, tiled=True)
    mine = lax.all_gather(mine, "vis", axis=2, tiled=True)
    real, imag = mine[0], mine[1]
    stacked = jnp.concatenate([real, imag], axis=1)
    rotated = jnp.concatenate([-imag, real], axis=1)
    input_total = input_count * inp_count
    row_count = input_total // vis_count
    left = lax.dynamic_slice_in_dim(stacked, vis_index * row_count, row_count, 2)
    re_block = jnp.einsum("cfa,cfb->cab", left, stacked, preferred_element_type=jnp.float32)
    im_block = jnp.einsum("cfa,cfb->cab", left, rotated, preferred_element_type=jnp.float32)
    row_ids = vis_index * row_count + jnp.arange(row_count, dtype=jnp.int32)
    col_ids = jnp.arange(input_total, dtype=jnp.int32)
    packed = jnp.where(col_ids[None, None, :] >= row_ids[None, :, None], re_block, im_block)
    return (packed / float(frame_count * vis_count)).astype(jnp.bfloat16)


def solution(mesh):
    def run(samples, history, fir_taps, kept_channels):
        input_count = samples.shape[1] // mesh.shape["inp"]
        row_count = samples.shape[1] // mesh.shape["vis"]
        one_channel = kept_channels.shape[0] == mesh.shape["inp"]
        frame_total, _, sample_total = samples.shape
        whole_tiles = input_count % LANES == 0 and row_count % COL_TILE == 0 and frame_total % 64 == 0
        binary = frame_total & (frame_total - 1) == 0 and sample_total & (sample_total - 1) == 0
        tiled = whole_tiles and binary and mesh.shape["vis"] == 4 and one_channel
        return jax.shard_map(
            per_device if tiled else per_device_plain,
            mesh=mesh,
            in_specs=(P("vis", "inp", None), P(None, "inp", None), P(), P()),
            out_specs=P("inp", "vis", None),
            check_vma=False,
        )(samples, history, fir_taps, kept_channels)

    return run
```

```python
import math

import jax
import jax.numpy as jnp
from jax import lax
from jax.experimental import pallas as pl
from jax.experimental.pallas import tpu as pltpu
from jax.sharding import PartitionSpec as P

TAPS = 4
CHUNK = 4
WINDOW = 3
HEAD = 16
LANES = 128
MIB = 1024 * 1024


def build_table(kept_ref, taps_ref, columns, wide):
    kept_total = kept_ref.shape[0]
    rows = 2 * kept_total
    count = taps_ref.shape[1]
    quarter = count // 4
    row_ids = lax.broadcasted_iota(jnp.int32, (kept_total, count), 0)
    positions = lax.broadcasted_iota(jnp.int32, (kept_total, count), 1)
    channels = jnp.zeros((kept_total, count), jnp.int32)
    for c in range(kept_total):
        channels = jnp.where(row_ids == c, kept_ref[c], channels)
    turns = (channels * positions) & (count - 1)
    quarters = (turns + quarter // 2) >> (quarter.bit_length() - 1)
    rest = (turns - quarters * quarter).astype(jnp.float32) * (2.0 * math.pi / count)
    square = rest * rest
    sine = rest * (1 + square * (-1 / 6 + square * (1 / 120 + square * (-1 / 5040 + square * (1 / 362880)))))
    cosine = 1 + square * (-1 / 2 + square * (1 / 24 + square * (-1 / 720 + square * (1 / 40320))))
    odd = (quarters & 1) == 1
    cos_part = jnp.where(odd, sine, cosine)
    sin_part = jnp.where(odd, cosine, sine)
    cos_part = jnp.where(((quarters + 1) & 2) == 2, -cos_part, cos_part)
    sin_part = jnp.where((quarters & 2) == 2, -sin_part, sin_part)
    norm_scale = 1.0 / math.sqrt(count)
    table = jnp.concatenate([cos_part * norm_scale, -sin_part * norm_scale], axis=0)
    table = table.astype(jnp.bfloat16).astype(jnp.float32)
    for place, tap in enumerate(reversed(range(TAPS))):
        scaled = table * taps_ref[tap : tap + 1, :]
        high = scaled.astype(jnp.bfloat16).astype(jnp.float32)
        columns[place * rows : (place + 1) * rows, :] = high
        columns[(TAPS + place) * rows : (TAPS + place + 1) * rows, :] = scaled - high

    for tile in range(count // LANES):
        part = slice(tile * LANES, (tile + 1) * LANES)
        wide[part, :] = columns[:, part].T.astype(jnp.bfloat16)


def spectra_kernel(
    kept_in, taps_in, samples_ref, history_ref, out_ref, held, columns, wide, sums, lines, products, kept, taps, sems, past_sem, kept_sem, taps_sem
):
    frame_count, input_count, sample_count = samples_ref.shape
    kept_total = kept_in.shape[0]
    rows = 2 * kept_total
    lead = TAPS - 1
    total = frame_count // CHUNK
    first_block = lax.axis_index("vis") == 0

    def chunk_copy(index):
        first = (total - 1 - index) * CHUNK
        return pltpu.make_async_copy(
            samples_ref.at[pl.ds(first, CHUNK)], held.at[pl.ds(first + CHUNK, CHUNK)], sems.at[index]
        )

    past_copy = pltpu.make_async_copy(history_ref, held.at[pl.ds(CHUNK - lead, lead)], past_sem)
    kept_copy = pltpu.make_async_copy(kept_in, kept, kept_sem)
    taps_copy = pltpu.make_async_copy(taps_in, taps, taps_sem)
    kept_copy.start()
    taps_copy.start()
    chunk_copy(0).start()
    products[...] = jnp.zeros_like(products)
    sums[...] = jnp.zeros_like(sums)
    kept_copy.wait()
    taps_copy.wait()
    for index in range(1, WINDOW):
        chunk_copy(index).start()

    build_table(kept, taps, columns, wide)

    stride = lines.shape[1] // rows

    def add_chunk(first, values):
        for k in reversed(range(CHUNK)):
            turned = values[k * input_count : (k + 1) * input_count].T
            both = turned[: TAPS * rows] + turned[TAPS * rows :]
            place = pl.ds(pl.multiple_of((first + k) * rows, 8), TAPS * rows)
            for h in range(input_count // LANES):
                added = sums[h, place, :] + both[:, h * LANES : (h + 1) * LANES]
                sums[h, place, :] = added
                lines[h, pl.ds(first + k + lead + 8 - CHUNK, rows, stride=stride), :] = added[lead * rows :]

    @pl.loop(0, total + jnp.where(first_block, 1, 0))
    def _(index):
        @pl.when(index < total)
        def _():
            chunk_copy(index).wait()

        @pl.when(index + WINDOW < total)
        def _():
            chunk_copy(index + WINDOW).start()

        @pl.when((index + WINDOW == total) & first_block)
        def _():
            past_copy.start()

        @pl.when(index == total)
        def _():
            past_copy.wait()

        first = (total - index) * CHUNK
        block = held[pl.ds(first, CHUNK)].reshape(CHUNK * input_count, sample_count)
        add_chunk(first + CHUNK, products[...])
        products[...] = jnp.dot(block, wide[...], preferred_element_type=jnp.float32)

    add_chunk(jnp.where(first_block, 0, CHUNK), products[...])
    for slot in range(lead):
        for h in range(input_count // LANES):
            done = sums[h, (CHUNK + slot) * rows : (CHUNK + slot + 1) * rows, :]
            lines[h, pl.ds(8 + slot, rows, stride=stride), :] = done

    halo_rows = lax.broadcasted_iota(jnp.int32, (8, LANES), 0)
    for c in range(kept_total):
        for h in range(input_count // LANES):
            cols = slice(h * LANES, (h + 1) * LANES)
            for part in range(2):
                first = (part * kept_total + c) * stride + 8
                column = lines[h, first : first + frame_count, :]
                out_ref[c, part * frame_count : (part + 1) * frame_count, cols] = column.astype(jnp.bfloat16)
            first = c * stride + 8 + frame_count
            real_tail = lines[h, first : first + 8, :]
            first += kept_total * stride
            imag_tail = pltpu.roll(lines[h, first : first + 8, :], lead, 0)
            tail = jnp.where(halo_rows < lead, real_tail, jnp.where(halo_rows < 2 * lead, imag_tail, 0.0))
            out_ref[c, 2 * frame_count :, cols] = tail.astype(jnp.bfloat16)


def spectra_part(samples, history, fir_taps, kept_channels):
    frame_count, input_count, sample_count = samples.shape
    kept_total = kept_channels.shape[0]
    rows = 2 * kept_total
    wide_count = 2 * TAPS * rows
    return pl.pallas_call(
        spectra_kernel,
        out_shape=jax.ShapeDtypeStruct((kept_total, 2 * frame_count + 8, input_count), jnp.bfloat16),
        in_specs=[pl.BlockSpec(memory_space=pl.ANY)] * 4,
        out_specs=pl.BlockSpec(memory_space=pltpu.VMEM),
        scratch_shapes=[
            pltpu.VMEM((frame_count + CHUNK, input_count, sample_count), jnp.bfloat16),
            pltpu.VMEM((wide_count, sample_count), jnp.float32),
            pltpu.VMEM((sample_count, wide_count), jnp.bfloat16),
            pltpu.VMEM((input_count // LANES, (frame_count + CHUNK + 8) * rows, LANES), jnp.float32),
            pltpu.VMEM((input_count // LANES, rows * (frame_count + 16), LANES), jnp.float32),
            pltpu.VMEM((CHUNK * input_count, wide_count), jnp.float32),
            pltpu.SMEM((kept_total,), jnp.int32),
            pltpu.VMEM((TAPS, sample_count), jnp.float32),
            pltpu.SemaphoreType.DMA((frame_count // CHUNK,)),
            pltpu.SemaphoreType.DMA,
            pltpu.SemaphoreType.DMA,
            pltpu.SemaphoreType.DMA,
        ],
        compiler_params=pltpu.CompilerParams(vmem_limit_bytes=62 * MIB),
    )(kept_channels, fir_taps, samples, history)


def correlate_kernel(
    own_ref, core_ref, near_ref, near_core_ref, cross_ref, cross_core_ref,
    out_ref, chip, far, halos, heads, left, tiles, sems, *, frame_count, scale,
):
    me = lax.axis_index("vis")
    here = lax.axis_index("inp")
    sources, _, input_count = own_ref.shape
    half_count = sources // 2
    for whole, near, cross in ((chip, near_ref, cross_ref), (far, near_core_ref, cross_core_ref)):
        for s in range(half_count):
            whole[here ^ s] = near[s]
            whole[half_count * (1 - here // half_count) + s] = cross[s]
    input_total = sources * input_count
    lead = TAPS - 1
    row_count = left.shape[1]
    parts = (own_ref, core_ref, chip, far)
    for k, part in enumerate(parts):
        halos[me ^ k] = part[:, 2 * frame_count :, :]
    halo_rows = lax.broadcasted_iota(jnp.int32, (8, input_count), 0)
    rest = jnp.zeros((8, input_count), jnp.float32)
    for k, part in enumerate(parts):
        block = me ^ k
        before = jnp.maximum(block - 1, 0)
        for s in range(sources):
            halo = jnp.where(block > 0, halos[before, s].astype(jnp.float32), 0.0)
            for r, turned in enumerate((halo, pltpu.roll(halo, 8 - lead, 0))):
                head = jnp.concatenate([jnp.where(halo_rows < lead, turned, 0.0), rest], axis=0)
                first = part[s, r * frame_count : r * frame_count + HEAD, :].astype(jnp.float32) + head
                heads[r, k, s] = first.astype(jnp.bfloat16)

    def gathered(r, source):
        pieces = []
        for k, part in enumerate(parts):
            pieces += [heads[r, k, source], part[source, r * frame_count + HEAD : (r + 1) * frame_count, :]]
        return jnp.concatenate(pieces, axis=0)

    corner = row_count // input_count
    half = frame_count * len(parts)
    for j in range(corner):
        rows = slice(j * input_count, (j + 1) * input_count)
        real = gathered(0, me * corner + j).T * scale
        imag = gathered(1, me * corner + j).T * scale
        left[0, rows, :half] = real
        left[0, rows, half:] = imag
        left[1, rows, :half] = imag
        left[1, rows, half:] = -real

    def tile_copy(t):
        source = lax.rem(me * corner + t, sources)
        cols = pl.ds(pl.multiple_of(source * input_count, input_count), input_count)
        return pltpu.make_async_copy(tiles.at[t], out_ref.at[0, :, cols], sems.at[t])

    for t in range(sources):
        below = (me * corner + t >= sources).astype(jnp.int32)
        source = lax.rem(me * corner + t, sources)
        right = jnp.concatenate([gathered(0, source), gathered(1, source)], axis=0)
        if t < corner:
            row_ids = lax.broadcasted_iota(jnp.int32, (row_count, input_count), 0)
            col_ids = lax.broadcasted_iota(jnp.int32, (row_count, input_count), 1) + t * input_count
            real = jnp.dot(left[0], right, preferred_element_type=jnp.float32)
            imag = jnp.dot(left[1], right, preferred_element_type=jnp.float32)
            products = jnp.where(col_ids >= row_ids, real, imag)
        else:
            products = jnp.dot(left[below], right, preferred_element_type=jnp.float32)
        tiles[t] = products.astype(jnp.bfloat16)
        tile_copy(t).start()
    for t in range(sources):
        tile_copy(t).wait()


def correlate_part(parts, frame_count, row_count, block_total):
    sources, line_count, input_count = parts[0].shape
    depth = 2 * frame_count * block_total
    scale = 1.0 / (frame_count * block_total)
    return pl.pallas_call(
        lambda *refs: correlate_kernel(*refs, frame_count=frame_count, scale=scale),
        out_shape=jax.ShapeDtypeStruct((1, row_count, sources * input_count), jnp.bfloat16),
        in_specs=[pl.BlockSpec(memory_space=pltpu.VMEM)] * len(parts),
        out_specs=pl.BlockSpec(memory_space=pl.ANY),
        scratch_shapes=[
            pltpu.VMEM((sources, line_count, input_count), jnp.bfloat16),
            pltpu.VMEM((sources, line_count, input_count), jnp.bfloat16),
            pltpu.VMEM((block_total, sources, 8, input_count), jnp.bfloat16),
            pltpu.VMEM((2, block_total, sources, HEAD, input_count), jnp.bfloat16),
            pltpu.VMEM((2, row_count, depth), jnp.bfloat16),
            pltpu.VMEM((sources, row_count, input_count), jnp.bfloat16),
            pltpu.SemaphoreType.DMA((sources,)),
        ],
        compiler_params=pltpu.CompilerParams(vmem_limit_bytes=32 * MIB),
    )(*parts)


def exchanged(value, distance):
    count = lax.axis_size("vis")
    return lax.ppermute(value, "vis", [(source, source ^ distance) for source in range(count)])


def sent_across(spectra, distance):
    inp_count, vis_count = lax.axis_size("inp"), lax.axis_size("vis")
    pairs = [
        (i * vis_count + v, (i ^ distance) * vis_count + (v ^ 2)) for i in range(inp_count) for v in range(vis_count)
    ]
    mine = lax.dynamic_index_in_dim(spectra, lax.axis_index("inp") ^ distance, 0, keepdims=False)
    return lax.ppermute(mine, ("inp", "vis"), pairs)


def per_device(samples, history, fir_taps, kept_channels):
    vis_count = lax.axis_size("vis")
    inp_count = lax.axis_size("inp")
    frame_count, input_count, _ = samples.shape
    half = inp_count // 2
    spectra = spectra_part(samples, history, fir_taps, kept_channels)
    near = [sent_across(spectra, distance) for distance in range(half)]
    own = lax.all_to_all(spectra, "inp", split_axis=0, concat_axis=0, tiled=True)
    away = half * (1 - lax.axis_index("inp") // half)
    cross = exchanged(lax.dynamic_slice_in_dim(own, away, half, 0), 2)
    core = exchanged(own, 1)
    near = jnp.stack(near)
    parts = (own, core, near, exchanged(near, 1), cross, exchanged(cross, 1))
    return correlate_part(parts, frame_count, input_count * inp_count // vis_count, vis_count)


def shifted(value, axis, steps):
    count = lax.axis_size(axis)
    initial, last = (max(0, -steps), min(count, count - steps))
    return lax.ppermute(value, axis, [(source, source + steps) for source in range(initial, last)])


def make_table(kept_channels, sample_count):
    positions = jnp.arange(sample_count, dtype=jnp.int32)
    products = kept_channels[:, None] * positions[None, :] % sample_count
    angles = products.astype(jnp.float32) * (2.0 * math.pi / sample_count)
    norm_scale = 1.0 / math.sqrt(sample_count)
    table = jnp.concatenate([jnp.cos(angles) * norm_scale, -jnp.sin(angles) * norm_scale], axis=0)
    return table.astype(jnp.bfloat16)


def per_device_plain(samples, history, fir_taps, kept_channels):
    vis_count = lax.axis_size("vis")
    vis_index = lax.axis_index("vis")
    inp_count = lax.axis_size("inp")
    frame_count, input_count, sample_count = samples.shape
    kept_total = kept_channels.shape[0]
    previous = shifted(samples[frame_count - TAPS + 1 :], "vis", 1)
    previous = jnp.where(vis_index == 0, history, previous)
    extended = jnp.concatenate([previous, samples], axis=0).astype(jnp.float32)
    weighted = fir_taps[0] * extended[0:frame_count]
    for tap in range(1, TAPS):
        weighted = weighted + fir_taps[tap] * extended[tap : tap + frame_count]
    spectra = jnp.einsum(
        "kn,fin->kfi",
        make_table(kept_channels, sample_count),
        weighted.astype(jnp.bfloat16),
        preferred_element_type=jnp.float32,
    ).astype(jnp.bfloat16)
    spectra = spectra.reshape(2, kept_total, frame_count, input_count)
    mine = lax.all_to_all(spectra, "inp", split_axis=1, concat_axis=3, tiled=True)
    mine = lax.all_gather(mine, "vis", axis=2, tiled=True)
    real, imag = mine[0], mine[1]
    stacked = jnp.concatenate([real, imag], axis=1)
    rotated = jnp.concatenate([-imag, real], axis=1)
    input_total = input_count * inp_count
    row_count = input_total // vis_count
    left = lax.dynamic_slice_in_dim(stacked, vis_index * row_count, row_count, 2)
    re_block = jnp.einsum("cfa,cfb->cab", left, stacked, preferred_element_type=jnp.float32)
    im_block = jnp.einsum("cfa,cfb->cab", left, rotated, preferred_element_type=jnp.float32)
    row_ids = vis_index * row_count + jnp.arange(row_count, dtype=jnp.int32)
    col_ids = jnp.arange(input_total, dtype=jnp.int32)
    packed = jnp.where(col_ids[None, None, :] >= row_ids[None, :, None], re_block, im_block)
    return (packed / float(frame_count * vis_count)).astype(jnp.bfloat16)


def solution(mesh):
    def run(samples, history, fir_taps, kept_channels):
        input_count = samples.shape[1] // mesh.shape["inp"]
        row_count = samples.shape[1] // mesh.shape["vis"]
        one_channel = kept_channels.shape[0] == mesh.shape["inp"]
        frame_total, _, sample_total = samples.shape
        whole_tiles = input_count % LANES == 0 and row_count % input_count == 0 and frame_total % 64 == 0
        binary = frame_total & (frame_total - 1) == 0 and sample_total & (sample_total - 1) == 0
        binary = binary and mesh.shape["inp"] & (mesh.shape["inp"] - 1) == 0
        tiled = whole_tiles and binary and mesh.shape["vis"] == 4 and one_channel
        return jax.shard_map(
            per_device if tiled else per_device_plain,
            mesh=mesh,
            in_specs=(P("vis", "inp", None), P(None, "inp", None), P(), P()),
            out_specs=P("inp", "vis", None),
            check_vma=False,
        )(samples, history, fir_taps, kept_channels)

    return run
```

```python
import math

import jax
import jax.numpy as jnp
from jax import lax
from jax.experimental import pallas as pl
from jax.experimental.pallas import tpu as pltpu
from jax.sharding import PartitionSpec as P

TAPS = 4
CHUNK = 4
WINDOW = 3
HEAD = 16
LANES = 128
MIB = 1024 * 1024


def build_table(kept_ref, taps_ref, columns, wide):
    kept_total = kept_ref.shape[0]
    rows = 2 * kept_total
    count = taps_ref.shape[1]
    quarter = count // 4
    row_ids = lax.broadcasted_iota(jnp.int32, (kept_total, count), 0)
    positions = lax.broadcasted_iota(jnp.int32, (kept_total, count), 1)
    channels = jnp.zeros((kept_total, count), jnp.int32)
    for c in range(kept_total):
        channels = jnp.where(row_ids == c, kept_ref[c], channels)
    turns = (channels * positions) & (count - 1)
    quarters = (turns + quarter // 2) >> (quarter.bit_length() - 1)
    rest = (turns - quarters * quarter).astype(jnp.float32) * (2.0 * math.pi / count)
    square = rest * rest
    sine = rest * (1 + square * (-1 / 6 + square * (1 / 120 + square * (-1 / 5040 + square * (1 / 362880)))))
    cosine = 1 + square * (-1 / 2 + square * (1 / 24 + square * (-1 / 720 + square * (1 / 40320))))
    odd = (quarters & 1) == 1
    cos_part = jnp.where(odd, sine, cosine)
    sin_part = jnp.where(odd, cosine, sine)
    cos_part = jnp.where(((quarters + 1) & 2) == 2, -cos_part, cos_part)
    sin_part = jnp.where((quarters & 2) == 2, -sin_part, sin_part)
    norm_scale = 1.0 / math.sqrt(count)
    table = jnp.concatenate([cos_part * norm_scale, -sin_part * norm_scale], axis=0)
    table = table.astype(jnp.bfloat16).astype(jnp.float32)
    for place, tap in enumerate(reversed(range(TAPS))):
        scaled = table * taps_ref[tap : tap + 1, :]
        high = scaled.astype(jnp.bfloat16).astype(jnp.float32)
        columns[place * rows : (place + 1) * rows, :] = high
        columns[(TAPS + place) * rows : (TAPS + place + 1) * rows, :] = scaled - high

    for tile in range(count // LANES):
        part = slice(tile * LANES, (tile + 1) * LANES)
        wide[part, :] = columns[:, part].T.astype(jnp.bfloat16)


def spectra_kernel(kept_in, taps_in, samples_ref, history_ref, out_ref, *refs):
    near_refs = refs[: out_ref.shape[0] // 2]
    held, columns, wide, sums, lines, products, kept, taps, sems, past_sem, kept_sem, taps_sem = refs[len(near_refs) :]
    frame_count, input_count, sample_count = samples_ref.shape
    kept_total = kept_in.shape[0]
    rows = 2 * kept_total
    lead = TAPS - 1
    total = frame_count // CHUNK
    first_block = lax.axis_index("vis") == 0

    def chunk_copy(index):
        first = (total - 1 - index) * CHUNK
        return pltpu.make_async_copy(
            samples_ref.at[pl.ds(first, CHUNK)], held.at[pl.ds(first + CHUNK, CHUNK)], sems.at[index]
        )

    past_copy = pltpu.make_async_copy(history_ref, held.at[pl.ds(CHUNK - lead, lead)], past_sem)
    kept_copy = pltpu.make_async_copy(kept_in, kept, kept_sem)
    taps_copy = pltpu.make_async_copy(taps_in, taps, taps_sem)
    kept_copy.start()
    taps_copy.start()
    chunk_copy(0).start()
    products[...] = jnp.zeros_like(products)
    sums[...] = jnp.zeros_like(sums)
    kept_copy.wait()
    taps_copy.wait()
    for index in range(1, WINDOW):
        chunk_copy(index).start()

    build_table(kept, taps, columns, wide)

    stride = lines.shape[1] // rows

    def add_chunk(first, values):
        for k in reversed(range(CHUNK)):
            turned = values[k * input_count : (k + 1) * input_count].T
            both = turned[: TAPS * rows] + turned[TAPS * rows :]
            place = pl.ds(pl.multiple_of((first + k) * rows, 8), TAPS * rows)
            for h in range(input_count // LANES):
                added = sums[h, place, :] + both[:, h * LANES : (h + 1) * LANES]
                sums[h, place, :] = added
                lines[h, pl.ds(first + k + lead + 8 - CHUNK, rows, stride=stride), :] = added[lead * rows :]

    @pl.loop(0, total + jnp.where(first_block, 1, 0))
    def _(index):
        @pl.when(index < total)
        def _():
            chunk_copy(index).wait()

        @pl.when(index + WINDOW < total)
        def _():
            chunk_copy(index + WINDOW).start()

        @pl.when((index + WINDOW == total) & first_block)
        def _():
            past_copy.start()

        @pl.when(index == total)
        def _():
            past_copy.wait()

        first = (total - index) * CHUNK
        block = held[pl.ds(first, CHUNK)].reshape(CHUNK * input_count, sample_count)
        add_chunk(first + CHUNK, products[...])
        products[...] = jnp.dot(block, wide[...], preferred_element_type=jnp.float32)

    add_chunk(jnp.where(first_block, 0, CHUNK), products[...])
    for slot in range(lead):
        for h in range(input_count // LANES):
            done = sums[h, (CHUNK + slot) * rows : (CHUNK + slot + 1) * rows, :]
            lines[h, pl.ds(8 + slot, rows, stride=stride), :] = done

    halo_rows = lax.broadcasted_iota(jnp.int32, (8, LANES), 0)
    for c in range(kept_total):
        for h in range(input_count // LANES):
            cols = slice(h * LANES, (h + 1) * LANES)
            for part in range(2):
                first = (part * kept_total + c) * stride + 8
                column = lines[h, first : first + frame_count, :]
                out_ref[c, part * frame_count : (part + 1) * frame_count, cols] = column.astype(jnp.bfloat16)
            first = c * stride + 8 + frame_count
            real_tail = lines[h, first : first + 8, :]
            first += kept_total * stride
            imag_tail = pltpu.roll(lines[h, first : first + 8, :], lead, 0)
            tail = jnp.where(halo_rows < lead, real_tail, jnp.where(halo_rows < 2 * lead, imag_tail, 0.0))
            out_ref[c, 2 * frame_count :, cols] = tail.astype(jnp.bfloat16)

    for distance, near_ref in enumerate(near_refs):
        near_ref[...] = out_ref[lax.axis_index("inp") ^ distance]


def spectra_part(samples, history, fir_taps, kept_channels):
    frame_count, input_count, sample_count = samples.shape
    kept_total = kept_channels.shape[0]
    rows = 2 * kept_total
    wide_count = 2 * TAPS * rows
    near = jax.ShapeDtypeStruct((2 * frame_count + 8, input_count), jnp.bfloat16)
    payload = jax.ShapeDtypeStruct((kept_total, *near.shape), jnp.bfloat16)
    return pl.pallas_call(
        spectra_kernel,
        out_shape=[payload] + [near] * (kept_total // 2),
        in_specs=[pl.BlockSpec(memory_space=pl.ANY)] * 4,
        out_specs=[pl.BlockSpec(memory_space=pltpu.VMEM)] * (1 + kept_total // 2),
        scratch_shapes=[
            pltpu.VMEM((frame_count + CHUNK, input_count, sample_count), jnp.bfloat16),
            pltpu.VMEM((wide_count, sample_count), jnp.float32),
            pltpu.VMEM((sample_count, wide_count), jnp.bfloat16),
            pltpu.VMEM((input_count // LANES, (frame_count + CHUNK + 8) * rows, LANES), jnp.float32),
            pltpu.VMEM((input_count // LANES, rows * (frame_count + 16), LANES), jnp.float32),
            pltpu.VMEM((CHUNK * input_count, wide_count), jnp.float32),
            pltpu.SMEM((kept_total,), jnp.int32),
            pltpu.VMEM((TAPS, sample_count), jnp.float32),
            pltpu.SemaphoreType.DMA((frame_count // CHUNK,)),
            pltpu.SemaphoreType.DMA,
            pltpu.SemaphoreType.DMA,
            pltpu.SemaphoreType.DMA,
        ],
        compiler_params=pltpu.CompilerParams(vmem_limit_bytes=62 * MIB),
    )(kept_channels, fir_taps, samples, history)


def correlate_kernel(
    own_ref, core_ref, near_ref, near_core_ref, cross_ref, cross_core_ref,
    out_ref, chip, far, halos, heads, left, tiles, sems, *, frame_count, scale,
):
    me = lax.axis_index("vis")
    here = lax.axis_index("inp")
    sources, _, input_count = own_ref.shape
    half_count = sources // 2
    for whole, near, cross in ((chip, near_ref, cross_ref), (far, near_core_ref, cross_core_ref)):
        for s in range(half_count):
            whole[here ^ s] = near[s]
            whole[half_count * (1 - here // half_count) + s] = cross[s]
    input_total = sources * input_count
    lead = TAPS - 1
    row_count = left.shape[1]
    parts = (own_ref, core_ref, chip, far)
    for k, part in enumerate(parts):
        halos[me ^ k] = part[:, 2 * frame_count :, :]
    halo_rows = lax.broadcasted_iota(jnp.int32, (8, input_count), 0)
    rest = jnp.zeros((8, input_count), jnp.float32)
    for k, part in enumerate(parts):
        block = me ^ k
        before = jnp.maximum(block - 1, 0)
        for s in range(sources):
            halo = jnp.where(block > 0, halos[before, s].astype(jnp.float32), 0.0)
            for r, turned in enumerate((halo, pltpu.roll(halo, 8 - lead, 0))):
                head = jnp.concatenate([jnp.where(halo_rows < lead, turned, 0.0), rest], axis=0)
                first = part[s, r * frame_count : r * frame_count + HEAD, :].astype(jnp.float32) + head
                heads[r, k, s] = first.astype(jnp.bfloat16)

    def gathered(r, source):
        pieces = []
        for k, part in enumerate(parts):
            pieces += [heads[r, k, source], part[source, r * frame_count + HEAD : (r + 1) * frame_count, :]]
        return jnp.concatenate(pieces, axis=0)

    corner = row_count // input_count
    half = frame_count * len(parts)
    for j in range(corner):
        rows = slice(j * input_count, (j + 1) * input_count)
        real = gathered(0, me * corner + j).T * scale
        imag = gathered(1, me * corner + j).T * scale
        left[0, rows, :half] = real
        left[0, rows, half:] = imag
        left[1, rows, :half] = imag
        left[1, rows, half:] = -real

    def tile_copy(t):
        source = lax.rem(me * corner + t, sources)
        cols = pl.ds(pl.multiple_of(source * input_count, input_count), input_count)
        return pltpu.make_async_copy(tiles.at[t], out_ref.at[0, :, cols], sems.at[t])

    for t in range(sources):
        below = (me * corner + t >= sources).astype(jnp.int32)
        source = lax.rem(me * corner + t, sources)
        right = jnp.concatenate([gathered(0, source), gathered(1, source)], axis=0)
        if t < corner:
            row_ids = lax.broadcasted_iota(jnp.int32, (row_count, input_count), 0)
            col_ids = lax.broadcasted_iota(jnp.int32, (row_count, input_count), 1) + t * input_count
            real = jnp.dot(left[0], right, preferred_element_type=jnp.float32)
            imag = jnp.dot(left[1], right, preferred_element_type=jnp.float32)
            products = jnp.where(col_ids >= row_ids, real, imag)
        else:
            products = jnp.dot(left[below], right, preferred_element_type=jnp.float32)
        tiles[t] = products.astype(jnp.bfloat16)
        tile_copy(t).start()
    for t in range(sources):
        tile_copy(t).wait()


def correlate_part(parts, frame_count, row_count, block_total):
    sources, line_count, input_count = parts[0].shape
    depth = 2 * frame_count * block_total
    scale = 1.0 / (frame_count * block_total)
    return pl.pallas_call(
        lambda *refs: correlate_kernel(*refs, frame_count=frame_count, scale=scale),
        out_shape=jax.ShapeDtypeStruct((1, row_count, sources * input_count), jnp.bfloat16),
        in_specs=[pl.BlockSpec(memory_space=pltpu.VMEM)] * len(parts),
        out_specs=pl.BlockSpec(memory_space=pl.ANY),
        scratch_shapes=[
            pltpu.VMEM((sources, line_count, input_count), jnp.bfloat16),
            pltpu.VMEM((sources, line_count, input_count), jnp.bfloat16),
            pltpu.VMEM((block_total, sources, 8, input_count), jnp.bfloat16),
            pltpu.VMEM((2, block_total, sources, HEAD, input_count), jnp.bfloat16),
            pltpu.VMEM((2, row_count, depth), jnp.bfloat16),
            pltpu.VMEM((sources, row_count, input_count), jnp.bfloat16),
            pltpu.SemaphoreType.DMA((sources,)),
        ],
        compiler_params=pltpu.CompilerParams(vmem_limit_bytes=32 * MIB),
    )(*parts)


def exchanged(value, distance):
    count = lax.axis_size("vis")
    return lax.ppermute(value, "vis", [(source, source ^ distance) for source in range(count)])


def sent_across(value, distance):
    inp_count, vis_count = lax.axis_size("inp"), lax.axis_size("vis")
    pairs = [
        (i * vis_count + v, (i ^ distance) * vis_count + (v ^ 2)) for i in range(inp_count) for v in range(vis_count)
    ]
    return lax.ppermute(value, ("inp", "vis"), pairs)


def per_device(samples, history, fir_taps, kept_channels):
    vis_count = lax.axis_size("vis")
    inp_count = lax.axis_size("inp")
    frame_count, input_count, _ = samples.shape
    half = inp_count // 2
    spectra, *near = spectra_part(samples, history, fir_taps, kept_channels)
    near = [sent_across(value, distance) for distance, value in enumerate(near)]
    own = lax.all_to_all(spectra, "inp", split_axis=0, concat_axis=0, tiled=True)
    away = half * (1 - lax.axis_index("inp") // half)
    cross = exchanged(lax.dynamic_slice_in_dim(own, away, half, 0), 2)
    core = exchanged(own, 1)
    near = jnp.stack(near)
    parts = (own, core, near, exchanged(near, 1), cross, exchanged(cross, 1))
    return correlate_part(parts, frame_count, input_count * inp_count // vis_count, vis_count)


def shifted(value, axis, steps):
    count = lax.axis_size(axis)
    initial, last = (max(0, -steps), min(count, count - steps))
    return lax.ppermute(value, axis, [(source, source + steps) for source in range(initial, last)])


def make_table(kept_channels, sample_count):
    positions = jnp.arange(sample_count, dtype=jnp.int32)
    products = kept_channels[:, None] * positions[None, :] % sample_count
    angles = products.astype(jnp.float32) * (2.0 * math.pi / sample_count)
    norm_scale = 1.0 / math.sqrt(sample_count)
    table = jnp.concatenate([jnp.cos(angles) * norm_scale, -jnp.sin(angles) * norm_scale], axis=0)
    return table.astype(jnp.bfloat16)


def per_device_plain(samples, history, fir_taps, kept_channels):
    vis_count = lax.axis_size("vis")
    vis_index = lax.axis_index("vis")
    inp_count = lax.axis_size("inp")
    frame_count, input_count, sample_count = samples.shape
    kept_total = kept_channels.shape[0]
    previous = shifted(samples[frame_count - TAPS + 1 :], "vis", 1)
    previous = jnp.where(vis_index == 0, history, previous)
    extended = jnp.concatenate([previous, samples], axis=0).astype(jnp.float32)
    weighted = fir_taps[0] * extended[0:frame_count]
    for tap in range(1, TAPS):
        weighted = weighted + fir_taps[tap] * extended[tap : tap + frame_count]
    spectra = jnp.einsum(
        "kn,fin->kfi",
        make_table(kept_channels, sample_count),
        weighted.astype(jnp.bfloat16),
        preferred_element_type=jnp.float32,
    ).astype(jnp.bfloat16)
    spectra = spectra.reshape(2, kept_total, frame_count, input_count)
    mine = lax.all_to_all(spectra, "inp", split_axis=1, concat_axis=3, tiled=True)
    mine = lax.all_gather(mine, "vis", axis=2, tiled=True)
    real, imag = mine[0], mine[1]
    stacked = jnp.concatenate([real, imag], axis=1)
    rotated = jnp.concatenate([-imag, real], axis=1)
    input_total = input_count * inp_count
    row_count = input_total // vis_count
    left = lax.dynamic_slice_in_dim(stacked, vis_index * row_count, row_count, 2)
    re_block = jnp.einsum("cfa,cfb->cab", left, stacked, preferred_element_type=jnp.float32)
    im_block = jnp.einsum("cfa,cfb->cab", left, rotated, preferred_element_type=jnp.float32)
    row_ids = vis_index * row_count + jnp.arange(row_count, dtype=jnp.int32)
    col_ids = jnp.arange(input_total, dtype=jnp.int32)
    packed = jnp.where(col_ids[None, None, :] >= row_ids[None, :, None], re_block, im_block)
    return (packed / float(frame_count * vis_count)).astype(jnp.bfloat16)


def solution(mesh):
    def run(samples, history, fir_taps, kept_channels):
        input_count = samples.shape[1] // mesh.shape["inp"]
        row_count = samples.shape[1] // mesh.shape["vis"]
        one_channel = kept_channels.shape[0] == mesh.shape["inp"]
        frame_total, _, sample_total = samples.shape
        whole_tiles = input_count % LANES == 0 and row_count % input_count == 0 and frame_total % 64 == 0
        binary = frame_total & (frame_total - 1) == 0 and sample_total & (sample_total - 1) == 0
        binary = binary and mesh.shape["inp"] & (mesh.shape["inp"] - 1) == 0
        tiled = whole_tiles and binary and mesh.shape["vis"] == 4 and one_channel
        return jax.shard_map(
            per_device if tiled else per_device_plain,
            mesh=mesh,
            in_specs=(P("vis", "inp", None), P(None, "inp", None), P(), P()),
            out_specs=P("inp", "vis", None),
            check_vma=False,
        )(samples, history, fir_taps, kept_channels)

    return run
```

```python
import math

import jax
import jax.numpy as jnp
from jax import lax
from jax.experimental import pallas as pl
from jax.experimental.pallas import tpu as pltpu
from jax.sharding import PartitionSpec as P

TAPS = 4
CHUNK = 4
WINDOW = 3
HEAD = 16
LANES = 128
MIB = 1024 * 1024


def build_table(kept_ref, taps_ref, columns, wide):
    kept_total = kept_ref.shape[0]
    rows = 2 * kept_total
    count = taps_ref.shape[1]
    quarter = count // 4
    row_ids = lax.broadcasted_iota(jnp.int32, (kept_total, count), 0)
    positions = lax.broadcasted_iota(jnp.int32, (kept_total, count), 1)
    channels = jnp.zeros((kept_total, count), jnp.int32)
    for c in range(kept_total):
        channels = jnp.where(row_ids == c, kept_ref[c], channels)
    turns = (channels * positions) & (count - 1)
    quarters = (turns + quarter // 2) >> (quarter.bit_length() - 1)
    rest = (turns - quarters * quarter).astype(jnp.float32) * (2.0 * math.pi / count)
    square = rest * rest
    sine = rest * (1 + square * (-1 / 6 + square * (1 / 120 + square * (-1 / 5040 + square * (1 / 362880)))))
    cosine = 1 + square * (-1 / 2 + square * (1 / 24 + square * (-1 / 720 + square * (1 / 40320))))
    odd = (quarters & 1) == 1
    cos_part = jnp.where(odd, sine, cosine)
    sin_part = jnp.where(odd, cosine, sine)
    cos_part = jnp.where(((quarters + 1) & 2) == 2, -cos_part, cos_part)
    sin_part = jnp.where((quarters & 2) == 2, -sin_part, sin_part)
    norm_scale = 1.0 / math.sqrt(count)
    table = jnp.concatenate([cos_part * norm_scale, -sin_part * norm_scale], axis=0)
    table = table.astype(jnp.bfloat16).astype(jnp.float32)
    for place, tap in enumerate(reversed(range(TAPS))):
        scaled = table * taps_ref[tap : tap + 1, :]
        high = scaled.astype(jnp.bfloat16).astype(jnp.float32)
        columns[place * rows : (place + 1) * rows, :] = high
        columns[(TAPS + place) * rows : (TAPS + place + 1) * rows, :] = scaled - high

    for tile in range(count // LANES):
        part = slice(tile * LANES, (tile + 1) * LANES)
        wide[part, :] = columns[:, part].T.astype(jnp.bfloat16)


def spectra_kernel(
    kept_in, taps_in, samples_ref, history_ref, out_ref, held, columns, wide, sums, lines, products, kept, taps, sems, past_sem, kept_sem, taps_sem
):
    frame_count, input_count, sample_count = samples_ref.shape
    kept_total = kept_in.shape[0]
    rows = 2 * kept_total
    lead = TAPS - 1
    total = frame_count // CHUNK
    first_block = lax.axis_index("vis") == 0

    def chunk_copy(index):
        first = (total - 1 - index) * CHUNK
        return pltpu.make_async_copy(
            samples_ref.at[pl.ds(first, CHUNK)], held.at[pl.ds(first + CHUNK, CHUNK)], sems.at[index]
        )

    past_copy = pltpu.make_async_copy(history_ref, held.at[pl.ds(CHUNK - lead, lead)], past_sem)
    kept_copy = pltpu.make_async_copy(kept_in, kept, kept_sem)
    taps_copy = pltpu.make_async_copy(taps_in, taps, taps_sem)
    kept_copy.start()
    taps_copy.start()
    chunk_copy(0).start()
    products[...] = jnp.zeros_like(products)
    sums[...] = jnp.zeros_like(sums)
    kept_copy.wait()
    taps_copy.wait()
    for index in range(1, WINDOW):
        chunk_copy(index).start()

    build_table(kept, taps, columns, wide)

    stride = lines.shape[1] // rows

    def add_chunk(first, values):
        for k in reversed(range(CHUNK)):
            turned = values[k * input_count : (k + 1) * input_count].T
            both = turned[: TAPS * rows] + turned[TAPS * rows :]
            place = pl.ds(pl.multiple_of((first + k) * rows, 8), TAPS * rows)
            for h in range(input_count // LANES):
                added = sums[h, place, :] + both[:, h * LANES : (h + 1) * LANES]
                sums[h, place, :] = added
                lines[h, pl.ds(first + k + lead + 8 - CHUNK, rows, stride=stride), :] = added[lead * rows :]

    @pl.loop(0, total + jnp.where(first_block, 1, 0))
    def _(index):
        @pl.when(index < total)
        def _():
            chunk_copy(index).wait()

        @pl.when(index + WINDOW < total)
        def _():
            chunk_copy(index + WINDOW).start()

        @pl.when((index + WINDOW == total) & first_block)
        def _():
            past_copy.start()

        @pl.when(index == total)
        def _():
            past_copy.wait()

        first = (total - index) * CHUNK
        block = held[pl.ds(first, CHUNK)].reshape(CHUNK * input_count, sample_count)
        add_chunk(first + CHUNK, products[...])
        products[...] = jnp.dot(block, wide[...], preferred_element_type=jnp.float32)

    add_chunk(jnp.where(first_block, 0, CHUNK), products[...])
    for slot in range(lead):
        for h in range(input_count // LANES):
            done = sums[h, (CHUNK + slot) * rows : (CHUNK + slot + 1) * rows, :]
            lines[h, pl.ds(8 + slot, rows, stride=stride), :] = done

    halo_rows = lax.broadcasted_iota(jnp.int32, (8, LANES), 0)
    for c in range(kept_total):
        for h in range(input_count // LANES):
            cols = slice(h * LANES, (h + 1) * LANES)
            for part in range(2):
                first = (part * kept_total + c) * stride + 8
                column = lines[h, first : first + frame_count, :]
                out_ref[c, part * frame_count : (part + 1) * frame_count, cols] = column.astype(jnp.bfloat16)
            first = c * stride + 8 + frame_count
            real_tail = lines[h, first : first + 8, :]
            first += kept_total * stride
            imag_tail = pltpu.roll(lines[h, first : first + 8, :], lead, 0)
            tail = jnp.where(halo_rows < lead, real_tail, jnp.where(halo_rows < 2 * lead, imag_tail, 0.0))
            out_ref[c, 2 * frame_count :, cols] = tail.astype(jnp.bfloat16)


def spectra_part(samples, history, fir_taps, kept_channels):
    frame_count, input_count, sample_count = samples.shape
    kept_total = kept_channels.shape[0]
    rows = 2 * kept_total
    wide_count = 2 * TAPS * rows
    return pl.pallas_call(
        spectra_kernel,
        out_shape=jax.ShapeDtypeStruct((kept_total, 2 * frame_count + 8, input_count), jnp.bfloat16),
        in_specs=[pl.BlockSpec(memory_space=pl.ANY)] * 4,
        out_specs=pl.BlockSpec(memory_space=pltpu.VMEM),
        scratch_shapes=[
            pltpu.VMEM((frame_count + CHUNK, input_count, sample_count), jnp.bfloat16),
            pltpu.VMEM((wide_count, sample_count), jnp.float32),
            pltpu.VMEM((sample_count, wide_count), jnp.bfloat16),
            pltpu.VMEM((input_count // LANES, (frame_count + CHUNK + 8) * rows, LANES), jnp.float32),
            pltpu.VMEM((input_count // LANES, rows * (frame_count + 16), LANES), jnp.float32),
            pltpu.VMEM((CHUNK * input_count, wide_count), jnp.float32),
            pltpu.SMEM((kept_total,), jnp.int32),
            pltpu.VMEM((TAPS, sample_count), jnp.float32),
            pltpu.SemaphoreType.DMA((frame_count // CHUNK,)),
            pltpu.SemaphoreType.DMA,
            pltpu.SemaphoreType.DMA,
            pltpu.SemaphoreType.DMA,
        ],
        compiler_params=pltpu.CompilerParams(vmem_limit_bytes=62 * MIB),
    )(kept_channels, fir_taps, samples, history)


def correlate_kernel(
    own_ref, core_ref, near_ref, near_core_ref, cross_ref, cross_core_ref,
    out_ref, chip, far, halos, heads, left, tiles, sems, *, frame_count, scale,
):
    me = lax.axis_index("vis")
    here = lax.axis_index("inp")
    sources, _, input_count = own_ref.shape
    half_count = sources // 2
    for whole, near, cross in ((chip, near_ref, cross_ref), (far, near_core_ref, cross_core_ref)):
        for s in range(half_count):
            whole[here ^ s] = near[s]
            whole[half_count * (1 - here // half_count) + s] = cross[s]
    input_total = sources * input_count
    lead = TAPS - 1
    row_count = left.shape[1]
    parts = (own_ref, core_ref, chip, far)
    for k, part in enumerate(parts):
        halos[me ^ k] = part[:, 2 * frame_count :, :]
    halo_rows = lax.broadcasted_iota(jnp.int32, (8, input_count), 0)
    rest = jnp.zeros((8, input_count), jnp.float32)
    for k, part in enumerate(parts):
        block = me ^ k
        before = jnp.maximum(block - 1, 0)
        for s in range(sources):
            halo = jnp.where(block > 0, halos[before, s].astype(jnp.float32), 0.0)
            for r, turned in enumerate((halo, pltpu.roll(halo, 8 - lead, 0))):
                head = jnp.concatenate([jnp.where(halo_rows < lead, turned, 0.0), rest], axis=0)
                first = part[s, r * frame_count : r * frame_count + HEAD, :].astype(jnp.float32) + head
                heads[r, k, s] = first.astype(jnp.bfloat16)

    def gathered(r, source):
        pieces = []
        for k, part in enumerate(parts):
            pieces += [heads[r, k, source], part[source, r * frame_count + HEAD : (r + 1) * frame_count, :]]
        return jnp.concatenate(pieces, axis=0)

    corner = row_count // input_count
    half = frame_count * len(parts)
    for j in range(corner):
        rows = slice(j * input_count, (j + 1) * input_count)
        real = gathered(0, me * corner + j).T * scale
        imag = gathered(1, me * corner + j).T * scale
        left[0, rows, :half] = real
        left[0, rows, half:] = imag
        left[1, rows, :half] = imag
        left[1, rows, half:] = -real

    def tile_copy(t):
        source = lax.rem(me * corner + t, sources)
        cols = pl.ds(pl.multiple_of(source * input_count, input_count), input_count)
        return pltpu.make_async_copy(tiles.at[t], out_ref.at[0, :, cols], sems.at[t])

    for t in [*range(corner, 2 * corner), *range(corner), *range(2 * corner, sources)]:
        below = (me * corner + t >= sources).astype(jnp.int32)
        source = lax.rem(me * corner + t, sources)
        right = jnp.concatenate([gathered(0, source), gathered(1, source)], axis=0)
        if t < corner:
            row_ids = lax.broadcasted_iota(jnp.int32, (row_count, input_count), 0)
            col_ids = lax.broadcasted_iota(jnp.int32, (row_count, input_count), 1) + t * input_count
            real = jnp.dot(left[0], right, preferred_element_type=jnp.float32)
            imag = jnp.dot(left[1], right, preferred_element_type=jnp.float32)
            products = jnp.where(col_ids >= row_ids, real, imag)
        else:
            products = jnp.dot(left[below], right, preferred_element_type=jnp.float32)
        tiles[t] = products.astype(jnp.bfloat16)
        tile_copy(t).start()
    for t in range(sources):
        tile_copy(t).wait()


def correlate_part(parts, frame_count, row_count, block_total):
    sources, line_count, input_count = parts[0].shape
    depth = 2 * frame_count * block_total
    scale = 1.0 / (frame_count * block_total)
    return pl.pallas_call(
        lambda *refs: correlate_kernel(*refs, frame_count=frame_count, scale=scale),
        out_shape=jax.ShapeDtypeStruct((1, row_count, sources * input_count), jnp.bfloat16),
        in_specs=[pl.BlockSpec(memory_space=pltpu.VMEM)] * len(parts),
        out_specs=pl.BlockSpec(memory_space=pl.ANY),
        scratch_shapes=[
            pltpu.VMEM((sources, line_count, input_count), jnp.bfloat16),
            pltpu.VMEM((sources, line_count, input_count), jnp.bfloat16),
            pltpu.VMEM((block_total, sources, 8, input_count), jnp.bfloat16),
            pltpu.VMEM((2, block_total, sources, HEAD, input_count), jnp.bfloat16),
            pltpu.VMEM((2, row_count, depth), jnp.bfloat16),
            pltpu.VMEM((sources, row_count, input_count), jnp.bfloat16),
            pltpu.SemaphoreType.DMA((sources,)),
        ],
        compiler_params=pltpu.CompilerParams(vmem_limit_bytes=32 * MIB),
    )(*parts)


def exchanged(value, distance):
    count = lax.axis_size("vis")
    return lax.ppermute(value, "vis", [(source, source ^ distance) for source in range(count)])


def sent_across(spectra, distance):
    inp_count, vis_count = lax.axis_size("inp"), lax.axis_size("vis")
    pairs = [
        (i * vis_count + v, (i ^ distance) * vis_count + (v ^ 2)) for i in range(inp_count) for v in range(vis_count)
    ]
    mine = lax.dynamic_index_in_dim(spectra, lax.axis_index("inp") ^ distance, 0, keepdims=False)
    return lax.ppermute(mine, ("inp", "vis"), pairs)


def per_device(samples, history, fir_taps, kept_channels):
    vis_count = lax.axis_size("vis")
    inp_count = lax.axis_size("inp")
    frame_count, input_count, _ = samples.shape
    half = inp_count // 2
    spectra = spectra_part(samples, history, fir_taps, kept_channels)
    near = [sent_across(spectra, distance) for distance in range(half)]
    own = lax.all_to_all(spectra, "inp", split_axis=0, concat_axis=0, tiled=True)
    away = half * (1 - lax.axis_index("inp") // half)
    cross = exchanged(lax.dynamic_slice_in_dim(own, away, half, 0), 2)
    core = exchanged(own, 1)
    near = jnp.stack(near)
    parts = (own, core, near, exchanged(near, 1), cross, exchanged(cross, 1))
    return correlate_part(parts, frame_count, input_count * inp_count // vis_count, vis_count)


def shifted(value, axis, steps):
    count = lax.axis_size(axis)
    initial, last = (max(0, -steps), min(count, count - steps))
    return lax.ppermute(value, axis, [(source, source + steps) for source in range(initial, last)])


def make_table(kept_channels, sample_count):
    positions = jnp.arange(sample_count, dtype=jnp.int32)
    products = kept_channels[:, None] * positions[None, :] % sample_count
    angles = products.astype(jnp.float32) * (2.0 * math.pi / sample_count)
    norm_scale = 1.0 / math.sqrt(sample_count)
    table = jnp.concatenate([jnp.cos(angles) * norm_scale, -jnp.sin(angles) * norm_scale], axis=0)
    return table.astype(jnp.bfloat16)


def per_device_plain(samples, history, fir_taps, kept_channels):
    vis_count = lax.axis_size("vis")
    vis_index = lax.axis_index("vis")
    inp_count = lax.axis_size("inp")
    frame_count, input_count, sample_count = samples.shape
    kept_total = kept_channels.shape[0]
    previous = shifted(samples[frame_count - TAPS + 1 :], "vis", 1)
    previous = jnp.where(vis_index == 0, history, previous)
    extended = jnp.concatenate([previous, samples], axis=0).astype(jnp.float32)
    weighted = fir_taps[0] * extended[0:frame_count]
    for tap in range(1, TAPS):
        weighted = weighted + fir_taps[tap] * extended[tap : tap + frame_count]
    spectra = jnp.einsum(
        "kn,fin->kfi",
        make_table(kept_channels, sample_count),
        weighted.astype(jnp.bfloat16),
        preferred_element_type=jnp.float32,
    ).astype(jnp.bfloat16)
    spectra = spectra.reshape(2, kept_total, frame_count, input_count)
    mine = lax.all_to_all(spectra, "inp", split_axis=1, concat_axis=3, tiled=True)
    mine = lax.all_gather(mine, "vis", axis=2, tiled=True)
    real, imag = mine[0], mine[1]
    stacked = jnp.concatenate([real, imag], axis=1)
    rotated = jnp.concatenate([-imag, real], axis=1)
    input_total = input_count * inp_count
    row_count = input_total // vis_count
    left = lax.dynamic_slice_in_dim(stacked, vis_index * row_count, row_count, 2)
    re_block = jnp.einsum("cfa,cfb->cab", left, stacked, preferred_element_type=jnp.float32)
    im_block = jnp.einsum("cfa,cfb->cab", left, rotated, preferred_element_type=jnp.float32)
    row_ids = vis_index * row_count + jnp.arange(row_count, dtype=jnp.int32)
    col_ids = jnp.arange(input_total, dtype=jnp.int32)
    packed = jnp.where(col_ids[None, None, :] >= row_ids[None, :, None], re_block, im_block)
    return (packed / float(frame_count * vis_count)).astype(jnp.bfloat16)


def solution(mesh):
    def run(samples, history, fir_taps, kept_channels):
        input_count = samples.shape[1] // mesh.shape["inp"]
        row_count = samples.shape[1] // mesh.shape["vis"]
        one_channel = kept_channels.shape[0] == mesh.shape["inp"]
        frame_total, _, sample_total = samples.shape
        whole_tiles = input_count % LANES == 0 and row_count % input_count == 0 and frame_total % 64 == 0
        binary = frame_total & (frame_total - 1) == 0 and sample_total & (sample_total - 1) == 0
        binary = binary and mesh.shape["inp"] & (mesh.shape["inp"] - 1) == 0
        tiled = whole_tiles and binary and mesh.shape["vis"] == 4 and one_channel
        return jax.shard_map(
            per_device if tiled else per_device_plain,
            mesh=mesh,
            in_specs=(P("vis", "inp", None), P(None, "inp", None), P(), P()),
            out_specs=P("inp", "vis", None),
            check_vma=False,
        )(samples, history, fir_taps, kept_channels)

    return run
```
